256 devices in a mesh: depth: 16 (over x, y), img: 16 (over z, core).
Axes of the slice: x: 4, y: 4, z: 8, core: 2. Of those that a mesh axis runs over, the one named last changes fastest.
Arguments:
- velocity: float32 [3, 128, 16, 256, 256], P(None, 'depth', 'img'), may hold values from -6 to 6
- emission: float32 [3, 8], replicated, may hold values from 0 to 2
- extinction: float32 [8], replicated, may hold values from 0.4 to 4
Outputs:
- picture: float32 [4, 16, 256, 256], P(None, 'img')
The draws below stay inside these ranges and needn't reach their ends.
All inputs are finite; a program needn't handle non-finite values.
Results may differ from the reference program's by a relative error of at most 0.0003.
Values sent between devices are 32-bit elements; how exact they have to be, the bound alone decides.
A program may use at most 128 MiB of HBM per device.

```python
import math
import jax
import jax.numpy as jnp
from jax import lax

CX = 256
CY = 256
KNOTS = 8
ROW_GROUPS = 16
TILES = 16
NX = 256
NY = 4096
NZ = 128


def block_levels(rng, extent, cuts, least, top_value):
    loudness, own = 1.0, jax.random.fold_in(rng, 6)
    for axis_at, blocks in cuts:
        draws = jnp.exp(jax.random.uniform(jax.random.fold_in(own, axis_at), (blocks,), jnp.float32, least / len(cuts), top_value / len(cuts)))
        loudness = loudness * jnp.repeat(draws, extent[axis_at] // blocks).reshape([-1 if axis == axis_at else 1 for axis in range(len(extent))])
    return loudness


def noise(rng, extent, spread, limit, split=(), dtype=jnp.bfloat16):
    values = jax.random.normal(rng, extent, jnp.float32) * spread
    if len(split) > 0:
        values = block_levels(rng, extent, split, -0.22, 0.18) * values
    return jnp.clip(values, min=-limit, max=limit).astype(dtype)


def setup_inputs(seed: int = 0) -> dict:
    streams_of = jax.random.split(jax.random.key(seed), 4)
    velocity = noise(streams_of[0], (3, NZ, TILES, CX, CY), 1.0, 6.0, ((1, 16), (2, 16)), jnp.float32)
    emission = jnp.clip(jax.random.uniform(streams_of[1], (3, KNOTS), jnp.float32, 0.0, 2.0), 0.0, 2.0)
    extinction = jnp.clip(jnp.exp(jax.random.uniform(streams_of[2], (KNOTS,), jnp.float32, math.log(0.4), math.log(4.0))), 0.4, 4.0)
    return dict(velocity=velocity, emission=emission, extinction=extinction)


def central(field, dim):
    ahead_cut = [slice(1, -1), slice(1, -1), slice(1, -1)]
    behind_cut = [slice(1, -1), slice(1, -1), slice(1, -1)]
    ahead_cut[dim] = slice(2, None)
    behind_cut[dim] = slice(None, -2)
    return (field[tuple(ahead_cut)] - field[tuple(behind_cut)]) * 0.5

def vorticity(padded):
    flow_x, flow_y, flow_z = (padded[0], padded[1], padded[2])
    curl_x = central(flow_z, 2) - central(flow_y, 0)
    curl_y = central(flow_x, 0) - central(flow_z, 1)
    curl_z = central(flow_y, 1) - central(flow_x, 2)
    return jnp.sqrt(curl_x * curl_x + curl_y * curl_y + curl_z * curl_z)

def render(strength, emission, extinction, depth_cells):
    slope_x = central(strength, 1)
    slope_y = central(strength, 2)
    slope_z = central(strength, 0)
    length = jnp.sqrt(slope_x * slope_x + slope_y * slope_y + slope_z * slope_z)
    shading = 0.3 + 0.7 * jnp.abs(0.48 * slope_x + 0.6 * slope_y + 0.64 * slope_z) / jnp.maximum(length, 1.0)
    interior = strength[1:-1, 1:-1, 1:-1]
    knot_count = emission.shape[1]
    levels = jnp.clip(interior, 0.0, 4.0) * ((knot_count - 1) / 4.0)
    knot_marks = jnp.arange(knot_count).astype(jnp.float32)
    weights = jnp.maximum(0.0, 1.0 - jnp.abs(levels[None] - knot_marks[:, None, None, None]))
    lookup = jnp.concatenate([emission, extinction[None]], axis=0)
    blended = jnp.einsum('ck,kzxy->czxy', lookup, weights, precision=lax.Precision.HIGHEST)
    optical = blended[3] / depth_cells
    running = jnp.cumsum(optical, axis=0)
    lit_share = jnp.exp(optical - running) * -jnp.expm1(-optical) * shading
    colour = lax.optimization_barrier(jnp.sum(blended[:3] * lit_share[None], axis=1))
    clearance = jnp.exp(-running[-1])
    return jnp.concatenate([colour, clearance[None]], axis=0)

def reference(velocity, emission, extinction):
    column_groups = TILES // ROW_GROUPS
    grid = velocity.reshape(3, NZ, column_groups, ROW_GROUPS, CX, CY)
    grid = jnp.transpose(grid, (0, 1, 2, 4, 3, 5)).reshape(3, NZ, NX, NY)
    padded = jnp.pad(grid, ((0, 0), (2, 2), (2, 2), (2, 2)))
    depth_place = jnp.arange(NZ + 2).astype(jnp.int32) - 1
    anchor = jnp.zeros((), jnp.int32)

    def one_block(tile):
        column_start = tile // ROW_GROUPS * CX
        row_start = tile % ROW_GROUPS * CY
        block = lax.dynamic_slice(padded, (anchor, anchor, column_start.astype(jnp.int32), row_start.astype(jnp.int32)), (3, NZ + 4, CX + 4, CY + 4))
        strength = vorticity(block)
        column_place = column_start - 1 + jnp.arange(CX + 2).astype(jnp.int32)
        row_place = row_start - 1 + jnp.arange(CY + 2).astype(jnp.int32)
        inside = ((depth_place >= 0) & (depth_place < NZ))[:, None, None]
        inside = inside & ((column_place >= 0) & (column_place < NX))[None, :, None]
        inside = inside & ((row_place >= 0) & (row_place < NY))[None, None, :]
        strength = jnp.where(inside, strength, 0.0)
        return render(strength, emission, extinction, NZ)
    blocks = lax.map(one_block, jnp.arange(TILES).astype(jnp.int32))
    merged = jnp.transpose(blocks, (1, 0, 2, 3))
    return jnp.concatenate([merged[:3], 1.0 - merged[3:]], axis=0)
```

```python
import functools

import jax
import jax.numpy as jnp
from jax import lax
from jax.experimental import pallas as pl
from jax.experimental.pallas import tpu as pltpu
from jax.sharding import PartitionSpec as P

F32 = jnp.float32
LANES = 128
SUB = 8
CHUNKS = 2
TINY = 1.2e-38


def kernel(
    vel, emi, ext, out,
    uxy, uz, st, pack_l, pack_r, rim_l, rim_r, spack_l, spack_r, srim_l, srim_r,
    part, parts, done,
    loc_sem, face_send, face_recv, rim_send, rim_recv,
    sface_send, sface_recv, srim_send, srim_recv,
    piece_send, piece_recv, done_send, done_recv, own_sem,
):
    depth = lax.axis_index("depth")
    img = lax.axis_index("img")
    depth_n = lax.axis_size("depth")
    img_n = lax.axis_size("img")
    cells = vel.shape[1]
    cols = vel.shape[2]
    per = cols // CHUNKS
    mine = per // depth_n
    tiles = per // SUB
    layers = cells * depth_n

    def local(c, h):
        if c == 2:
            dst = uz.at[:, h, pl.ds(SUB, cols), :]
        else:
            dst = uxy.at[c, pl.ds(1, cells), h, pl.ds(SUB, cols), :]
        return pltpu.make_async_copy(
            vel.at[c, :, :, pl.ds(h * LANES, LANES)], dst, loc_sem.at[c, h]
        )

    for c in (0, 2, 1):
        for h in range(2):
            local(c, h).start()

    barrier = pltpu.get_barrier_semaphore()

    def greet(j, carry):
        peer = lax.rem(depth + j, depth_n)
        pl.semaphore_signal(barrier, inc=1, device_id={"depth": peer, "img": img})
        return carry

    lax.fori_loop(1, depth_n, greet, 0)

    for step in (1, img_n - 1):
        beside = lax.rem(img + step, img_n)
        pl.semaphore_signal(barrier, inc=1, device_id={"depth": depth, "img": beside})

    zero_tile = jnp.zeros((SUB, LANES), F32)
    for z in range(cells):
        for h in range(2):
            for at in (0, cols + SUB):
                uxy[1, z + 1, h, pl.ds(at, SUB), :] = zero_tile
                uz[z, h, pl.ds(at, SUB), :] = zero_tile
                st[z + 1, h, pl.ds(at, SUB), :] = zero_tile

    pl.semaphore_wait(barrier, depth_n + 1)

    def to_depth(peer):
        return {"depth": peer, "img": img}

    def to_img(peer):
        return {"depth": depth, "img": peer}

    def face(way, k, h):
        layer, slot, peer = ((cells - 1, 0, depth + 1), (0, cells + 1, depth - 1))[way]
        return pltpu.make_async_remote_copy(
            src_ref=vel.at[pl.ds(0, 2), layer, pl.ds(k * per, per), pl.ds(h * LANES, LANES)],
            dst_ref=uxy.at[pl.ds(0, 2), slot, h, pl.ds(SUB + k * per, per), :],
            send_sem=face_send.at[way, k, h],
            recv_sem=face_recv.at[way, k, h],
            device_id=to_depth(peer),
        )

    def strength_face(way, k):
        layer, slot, peer = ((cells, 0, depth + 1), (1, cells + 1, depth - 1))[way]
        rows = pl.ds(SUB + k * per, per)
        return pltpu.make_async_remote_copy(
            src_ref=st.at[layer, :, rows, :],
            dst_ref=st.at[slot, :, rows, :],
            send_sem=sface_send.at[way, k],
            recv_sem=sface_recv.at[way, k],
            device_id=to_depth(peer),
        )

    def rim(way):
        src, dst, peer = ((pack_r, rim_l, img + 1), (pack_l, rim_r, img - 1))[way]
        return pltpu.make_async_remote_copy(
            src_ref=src, dst_ref=dst,
            send_sem=rim_send.at[way], recv_sem=rim_recv.at[way],
            device_id=to_img(peer),
        )

    def strength_rim(way, k):
        src, dst, peer = ((spack_r, srim_l, img + 1), (spack_l, srim_r, img - 1))[way]
        rows = pl.ds(k * per, per)
        return pltpu.make_async_remote_copy(
            src_ref=src.at[rows, :], dst_ref=dst.at[rows, :],
            send_sem=srim_send.at[way, k], recv_sem=srim_recv.at[way, k],
            device_id=to_img(peer),
        )

    has_depth = (depth < depth_n - 1, depth > 0)
    from_depth = (depth > 0, depth < depth_n - 1)
    has_img = (img < img_n - 1, img > 0)
    from_img = (img > 0, img < img_n - 1)

    for k in range(CHUNKS):
        for way in range(2):
            @pl.when(has_depth[way])
            def _(way=way, k=k):
                for h in range(2):
                    face(way, k, h).start()

    lane = lax.broadcasted_iota(jnp.int32, (SUB, LANES), 1)
    first = lane == 0
    last = lane == LANES - 1

    def collect(tile, fields, dst_l, dst_r):
        low = zero_tile
        high = zero_tile
        for at, (v0, v1) in enumerate(fields):
            low = jnp.where(lane == at, v0 if at == 0 else pltpu.roll(v0, at, 1), low)
            high = jnp.where(lane == at, pltpu.roll(v1, at + 1, 1), high)
        rows = pl.ds(pl.multiple_of(tile * SUB, SUB), SUB)
        dst_l[rows, :] = low
        dst_r[rows, :] = high

    for h in range(2):
        local(0, h).wait()
        local(2, h).wait()

    def pack_flow(tile, carry):
        rows = pl.ds(pl.multiple_of(tile * SUB + SUB, SUB), SUB)
        fields = [(uxy[0, z + 1, 0, rows, :], uxy[0, z + 1, 1, rows, :]) for z in range(cells)]
        fields += [(uz[z, 0, rows, :], uz[z, 1, rows, :]) for z in range(cells)]
        collect(tile, fields, pack_l, pack_r)
        return carry

    lax.fori_loop(0, cols // SUB, pack_flow, 0)
    for way in range(2):
        @pl.when(has_img[way])
        def _(way=way):
            rim(way).start()

    for h in range(2):
        local(1, h).wait()
    for way, dst in ((0, rim_l), (1, rim_r)):
        @pl.when(from_img[way])
        def _(way=way):
            rim(way).wait_recv()

        @pl.when(jnp.logical_not(from_img[way]))
        def _(dst=dst):
            dst[...] = jnp.zeros(dst.shape, F32)

    def along_row(v0, v1, left, right):
        p0, p1 = pltpu.roll(v0, LANES - 1, 1), pltpu.roll(v1, LANES - 1, 1)
        m0, m1 = pltpu.roll(v0, 1, 1), pltpu.roll(v1, 1, 1)
        d0 = jnp.where(last, p1, p0) - jnp.where(first, left, m0)
        d1 = jnp.where(last, right, p1) - jnp.where(first, m0, m1)
        return d0, d1

    def edges(tile_l, tile_r, at):
        left = tile_l if at == 0 else pltpu.roll(tile_l, LANES - at, 1)
        right = pltpu.roll(tile_r, LANES - 1 - at, 1)
        return left, right

    def strength_tile(tile, zs):
        base = pl.multiple_of(tile * SUB, SUB)
        rows = pl.ds(pl.multiple_of(base + SUB, SUB), SUB)
        ahead = pl.ds(base + SUB + 1, SUB)
        behind = pl.ds(base + SUB - 1, SUB)
        tile_l, tile_r = rim_l[pl.ds(base, SUB), :], rim_r[pl.ds(base, SUB), :]
        for z in zs:
            dy_ux = along_row(
                uxy[0, z + 1, 0, rows, :], uxy[0, z + 1, 1, rows, :], *edges(tile_l, tile_r, z)
            )
            dy_uz = along_row(
                uz[z, 0, rows, :], uz[z, 1, rows, :], *edges(tile_l, tile_r, cells + z)
            )
            for h in range(2):
                dz_uy = uxy[1, z + 2, h, rows, :] - uxy[1, z, h, rows, :]
                dz_ux = uxy[0, z + 2, h, rows, :] - uxy[0, z, h, rows, :]
                dx_uz = uz[z, h, ahead, :] - uz[z, h, behind, :]
                dx_uy = uxy[1, z + 1, h, ahead, :] - uxy[1, z + 1, h, behind, :]
                cx = dy_uz[h] - dz_uy
                cy = dz_ux - dx_uz
                cz = dx_uy - dy_ux[h]
                square = cx * cx + cy * cy + cz * cz
                st[z + 1, h, rows, :] = square * (0.5 * lax.rsqrt(jnp.maximum(square, TINY)))

    def inner(tile, carry):
        strength_tile(tile, range(1, cells - 1))
        return carry

    lax.fori_loop(0, cols // SUB, inner, 0)

    def outer(tile, carry):
        strength_tile(tile, (0, cells - 1))
        rows = pl.ds(pl.multiple_of(tile * SUB + SUB, SUB), SUB)
        fields = [(st[z + 1, 0, rows, :], st[z + 1, 1, rows, :]) for z in range(cells)]
        collect(tile, fields, spack_l, spack_r)
        return carry

    for k in range(CHUNKS):
        for way, slot in ((0, 0), (1, cells + 1)):
            @pl.when(from_depth[way])
            def _(way=way, k=k):
                for h in range(2):
                    face(way, k, h).wait_recv()

            @pl.when(jnp.logical_not(from_depth[way]))
            def _(slot=slot, k=k):
                for h in range(2):
                    rows = pl.ds(SUB + k * per, per)
                    for c in range(2):
                        uxy[c, slot, h, rows, :] = jnp.zeros((per, LANES), F32)
                    st[slot, h, rows, :] = jnp.zeros((per, LANES), F32)

        lax.fori_loop(k * tiles, (k + 1) * tiles, outer, 0)
        for way in range(2):
            @pl.when(has_depth[way])
            def _(way=way, k=k):
                strength_face(way, k).start()

            @pl.when(has_img[way])
            def _(way=way, k=k):
                strength_rim(way, k).start()

    knots = ext.shape[0]

    def hinges(read):
        steps = [read(k + 1) - read(k) for k in range(knots - 1)]
        return [read(0), steps[0]] + [steps[k] - steps[k - 1] for k in range(1, knots - 1)]

    dense = [g * (1.0 / layers) for g in hinges(lambda k: ext[k])]
    tints = [hinges(lambda k, c=c: emi[c, k]) for c in range(3)]

    def shade(tile, carry):
        base = pl.multiple_of(tile * SUB, SUB)
        here = pl.ds(base, SUB)
        rows = pl.ds(pl.multiple_of(base + SUB, SUB), SUB)
        ahead = pl.ds(base + SUB + 1, SUB)
        behind = pl.ds(base + SUB - 1, SUB)
        tile_l, tile_r = srim_l[here, :], srim_r[here, :]
        clear = [jnp.ones((SUB, LANES), F32)] * 2
        sums = [[None] * knots for _ in range(2)]
        for z in range(cells):
            mid = [st[z + 1, h, rows, :] for h in range(2)]
            dy = along_row(mid[0], mid[1], *edges(tile_l, tile_r, z))
            for h in range(2):
                dx = st[z + 1, h, ahead, :] - st[z + 1, h, behind, :]
                dz = st[z + 2, h, rows, :] - st[z, h, rows, :]
                square = dx * dx + dy[h] * dy[h] + dz * dz
                lean = jnp.abs(0.48 * dx + 0.6 * dy[h] + 0.64 * dz)
                shading = 0.3 + 0.7 * lean * lax.rsqrt(jnp.maximum(square, 4.0))
                level = jnp.minimum(mid[h], 4.0) * ((knots - 1) / 4.0)
                bends = [level] + [jnp.maximum(level - k, 0.0) for k in range(1, knots - 1)]
                optical = dense[0] + dense[1] * level
                for k in range(1, knots - 1):
                    optical = optical + dense[k + 1] * bends[k]
                loss = optical * (
                    1.0 - optical * (0.5 - optical * (1.0 / 6.0 - optical * (1.0 / 24.0)))
                )
                taken = clear[h] * loss
                clear[h] = clear[h] - taken
                lit = taken * shading
                terms = [lit] + [lit * b for b in bends]
                for n in range(knots):
                    sums[h][n] = terms[n] if z == 0 else sums[h][n] + terms[n]
        for h in range(2):
            at = pl.ds(h * LANES, LANES)
            for c in range(3):
                colour = tints[c][0] * sums[h][0]
                for n in range(1, knots):
                    colour = colour + tints[c][n] * sums[h][n]
                part[c, here, at] = colour
            part[3, here, at] = clear[h]
        return carry

    def owned(k, who):
        return pl.ds(pl.multiple_of(k * per + who * mine, SUB), mine)

    def piece(k, to, slot):
        return pltpu.make_async_remote_copy(
            src_ref=part.at[:, owned(k, to), :],
            dst_ref=parts.at[k, slot],
            send_sem=piece_send.at[k, to],
            recv_sem=piece_recv.at[k, slot],
            device_id=to_depth(to),
        )

    def finished(k, to, who):
        return pltpu.make_async_remote_copy(
            src_ref=done.at[k],
            dst_ref=out.at[:, owned(k, who), :],
            send_sem=done_send.at[k, to],
            recv_sem=done_recv.at[k, who],
            device_id=to_depth(to),
        )

    def each_peer(act):
        def step(j, carry):
            act(lax.rem(depth + j, depth_n))
            return carry

        lax.fori_loop(1, depth_n, step, 0)

    for k in range(CHUNKS):
        for way, dst in ((0, srim_l), (1, srim_r)):
            @pl.when(from_depth[way])
            def _(way=way, k=k):
                strength_face(way, k).wait_recv()

            @pl.when(from_img[way])
            def _(way=way, k=k):
                strength_rim(way, k).wait_recv()

            @pl.when(jnp.logical_not(from_img[way]))
            def _(dst=dst, k=k):
                dst[pl.ds(k * per, per), :] = jnp.zeros((per, LANES), F32)

        lax.fori_loop(k * tiles, (k + 1) * tiles, shade, 0)
        each_peer(lambda peer, k=k: piece(k, peer, depth).start())
        parts[k, depth] = part[:, owned(k, depth), :]

    def own(k):
        return pltpu.make_async_copy(done.at[k], out.at[:, owned(k, depth), :], own_sem.at[k])

    for k in range(CHUNKS):
        each_peer(lambda peer, k=k: piece(k, depth, peer).wait_recv())

        def over(s, carry, k=k):
            red, green, blue, clear = carry
            red = red + clear * parts[k, s, 0]
            green = green + clear * parts[k, s, 1]
            blue = blue + clear * parts[k, s, 2]
            return red, green, blue, clear * parts[k, s, 3]

        none = jnp.zeros((mine, part.shape[2]), F32)
        red, green, blue, clear = lax.fori_loop(
            0, depth_n, over, (none, none, none, none + 1.0)
        )
        done[k, 0] = red
        done[k, 1] = green
        done[k, 2] = blue
        done[k, 3] = 1.0 - clear
        each_peer(lambda peer, k=k: finished(k, peer, depth).start())
        own(k).start()

    for k in range(CHUNKS):
        each_peer(lambda peer, k=k: finished(k, depth, peer).wait_recv())
        own(k).wait()

    for k in range(CHUNKS):
        for way in range(2):
            @pl.when(has_depth[way])
            def _(way=way, k=k):
                for h in range(2):
                    face(way, k, h).wait_send()
                strength_face(way, k).wait_send()

            @pl.when(has_img[way])
            def _(way=way, k=k):
                if k == 0:
                    rim(way).wait_send()
                strength_rim(way, k).wait_send()

        def sent(peer, k=k):
            piece(k, peer, depth).wait_send()
            finished(k, peer, depth).wait_send()

        each_peer(sent)


def shards(velocity, emission, extinction):
    flow = velocity[:, :, 0]
    _, cells, cols, rows = flow.shape
    depth_n = lax.axis_size("depth")
    per = cols // CHUNKS
    mine = per // depth_n
    tall = cols + 2 * SUB
    dma = pltpu.SemaphoreType.DMA
    picture = pl.pallas_call(
        kernel,
        out_shape=jax.ShapeDtypeStruct((4, cols, rows), F32),
        in_specs=[
            pl.BlockSpec(memory_space=pl.ANY),
            pl.BlockSpec(memory_space=pltpu.SMEM),
            pl.BlockSpec(memory_space=pltpu.SMEM),
        ],
        out_specs=pl.BlockSpec(memory_space=pl.ANY),
        scratch_shapes=[
            pltpu.VMEM((2, cells + 2, 2, tall, LANES), F32),
            pltpu.VMEM((cells, 2, tall, LANES), F32),
            pltpu.VMEM((cells + 2, 2, tall, LANES), F32),
        ]
        + [pltpu.VMEM((cols, LANES), F32) for _ in range(8)]
        + [
            pltpu.VMEM((4, cols, rows), F32),
            pltpu.VMEM((CHUNKS, depth_n, 4, mine, rows), F32),
            pltpu.VMEM((CHUNKS, 4, mine, rows), F32),
            dma((3, 2)),
            dma((2, CHUNKS, 2)),
            dma((2, CHUNKS, 2)),
            dma((2,)),
            dma((2,)),
            dma((2, CHUNKS)),
            dma((2, CHUNKS)),
            dma((2, CHUNKS)),
            dma((2, CHUNKS)),
            dma((CHUNKS, depth_n)),
            dma((CHUNKS, depth_n)),
            dma((CHUNKS, depth_n)),
            dma((CHUNKS, depth_n)),
            dma((CHUNKS,)),
        ],
        compiler_params=pltpu.CompilerParams(
            collective_id=0, has_side_effects=True, vmem_limit_bytes=48 * 1024 * 1024
        ),
        cost_estimate=pl.CostEstimate(
            flops=100 * cells * cols * rows, bytes_accessed=8 * 1024 * 1024, transcendentals=0
        ),
        name="render",
    )(flow, emission, extinction)
    return picture[:, None]


def solution(mesh):
    return jax.shard_map(
        shards,
        mesh=mesh,
        in_specs=(P(None, "depth", "img", None, None), P(), P()),
        out_specs=P(None, "img", None, None),
        check_vma=False,
    )
```

```python
import functools

import jax
import jax.numpy as jnp
from jax import lax
from jax.experimental import pallas as pl
from jax.experimental.pallas import tpu as pltpu
from jax.sharding import PartitionSpec as P

F32 = jnp.float32
LANES = 128
SUB = 8
CHUNKS = 4
SIDE = 4
TINY = 1.2e-38


def kernel(
    vel, emi_hbm, ext_hbm, out,
    uxy, uz, st, pack_l, pack_r, rim_l, rim_r, spack_l, spack_r, srim_l, srim_r,
    part, row_parts, row_sum, col_parts, done, emi, ext,
    table_sem, loc_sem, face_send, face_recv, rim_send, rim_recv,
    sface_send, sface_recv, srim_send, srim_recv,
    row_send, row_recv, col_send, col_recv, near_send, near_recv, far_send, far_recv, own_sem,
):
    depth = lax.axis_index("depth")
    img = lax.axis_index("img")
    depth_n = lax.axis_size("depth")
    img_n = lax.axis_size("img")
    cells = vel.shape[1]
    cols = vel.shape[2]
    per = cols // CHUNKS
    gx, gy = depth // SIDE, lax.rem(depth, SIDE)
    tiles = per // SUB
    layers = cells * depth_n

    def local(c, h):
        if c == 2:
            dst = uz.at[:, h, pl.ds(SUB, cols), :]
        else:
            dst = uxy.at[c, pl.ds(1, cells), h, pl.ds(SUB, cols), :]
        return pltpu.make_async_copy(
            vel.at[c, :, :, pl.ds(h * LANES, LANES)], dst, loc_sem.at[c, h]
        )

    for c in (0, 2, 1):
        for h in range(2):
            local(c, h).start()
    tables = [
        pltpu.make_async_copy(emi_hbm, emi, table_sem.at[0]),
        pltpu.make_async_copy(ext_hbm, ext, table_sem.at[1]),
    ]
    for table in tables:
        table.start()

    barrier = pltpu.get_barrier_semaphore()

    def greet(j, carry):
        peer = lax.rem(depth + j, depth_n)
        pl.semaphore_signal(barrier, inc=1, device_id={"depth": peer, "img": img})
        return carry

    lax.fori_loop(1, depth_n, greet, 0)

    for step in (1, img_n - 1):
        beside = lax.rem(img + step, img_n)
        pl.semaphore_signal(barrier, inc=1, device_id={"depth": depth, "img": beside})

    zero_tile = jnp.zeros((SUB, LANES), F32)
    for z in range(cells):
        for h in range(2):
            for at in (0, cols + SUB):
                uxy[1, z + 1, h, pl.ds(at, SUB), :] = zero_tile
                uz[z, h, pl.ds(at, SUB), :] = zero_tile
                st[z + 1, h, pl.ds(at, SUB), :] = zero_tile

    pl.semaphore_wait(barrier, depth_n + 1)

    def to_depth(peer):
        return {"depth": peer, "img": img}

    def to_img(peer):
        return {"depth": depth, "img": peer}

    def face(way, k, h):
        layer, slot, peer = ((cells - 1, 0, depth + 1), (0, cells + 1, depth - 1))[way]
        return pltpu.make_async_remote_copy(
            src_ref=vel.at[pl.ds(0, 2), layer, pl.ds(k * per, per), pl.ds(h * LANES, LANES)],
            dst_ref=uxy.at[pl.ds(0, 2), slot, h, pl.ds(SUB + k * per, per), :],
            send_sem=face_send.at[way, k, h],
            recv_sem=face_recv.at[way, k, h],
            device_id=to_depth(peer),
        )

    def strength_face(way, k):
        layer, slot, peer = ((cells, 0, depth + 1), (1, cells + 1, depth - 1))[way]
        rows = pl.ds(SUB + k * per, per)
        return pltpu.make_async_remote_copy(
            src_ref=st.at[layer, :, rows, :],
            dst_ref=st.at[slot, :, rows, :],
            send_sem=sface_send.at[way, k],
            recv_sem=sface_recv.at[way, k],
            device_id=to_depth(peer),
        )

    def rim(way, k):
        src, dst, peer = ((pack_r, rim_l, img + 1), (pack_l, rim_r, img - 1))[way]
        rows = pl.ds(k * per, per)
        return pltpu.make_async_remote_copy(
            src_ref=src.at[rows, :], dst_ref=dst.at[rows, :],
            send_sem=rim_send.at[way, k], recv_sem=rim_recv.at[way, k],
            device_id=to_img(peer),
        )

    def strength_rim(way, k):
        src, dst, peer = ((spack_r, srim_l, img + 1), (spack_l, srim_r, img - 1))[way]
        rows = pl.ds(k * per, per)
        return pltpu.make_async_remote_copy(
            src_ref=src.at[rows, :], dst_ref=dst.at[rows, :],
            send_sem=srim_send.at[way, k], recv_sem=srim_recv.at[way, k],
            device_id=to_img(peer),
        )

    has_depth = (depth < depth_n - 1, depth > 0)
    from_depth = (depth > 0, depth < depth_n - 1)
    has_img = (img < img_n - 1, img > 0)
    from_img = (img > 0, img < img_n - 1)

    for k in range(CHUNKS):
        for way in range(2):
            @pl.when(has_depth[way])
            def _(way=way, k=k):
                for h in range(2):
                    face(way, k, h).start()

    lane = lax.broadcasted_iota(jnp.int32, (SUB, LANES), 1)
    first = lane == 0
    last = lane == LANES - 1

    def collect(tile, fields, dst_l, dst_r):
        low = zero_tile
        high = zero_tile
        for at, (v0, v1) in enumerate(fields):
            low = jnp.where(lane == at, v0 if at == 0 else pltpu.roll(v0, at, 1), low)
            high = jnp.where(lane == at, pltpu.roll(v1, at + 1, 1), high)
        rows = pl.ds(pl.multiple_of(tile * SUB, SUB), SUB)
        dst_l[rows, :] = low
        dst_r[rows, :] = high

    for h in range(2):
        local(0, h).wait()
        local(2, h).wait()

    def pack_flow(tile, carry):
        rows = pl.ds(pl.multiple_of(tile * SUB + SUB, SUB), SUB)
        fields = [(uxy[0, z + 1, 0, rows, :], uxy[0, z + 1, 1, rows, :]) for z in range(cells)]
        fields += [(uz[z, 0, rows, :], uz[z, 1, rows, :]) for z in range(cells)]
        collect(tile, fields, pack_l, pack_r)
        return carry

    for k in range(CHUNKS):
        lax.fori_loop(k * tiles, (k + 1) * tiles, pack_flow, 0, unroll=4)
        for way in range(2):
            @pl.when(has_img[way])
            def _(way=way, k=k):
                rim(way, k).start()

    for h in range(2):
        local(1, h).wait()

    def along_row(v0, v1, left, right):
        p0, p1 = pltpu.roll(v0, LANES - 1, 1), pltpu.roll(v1, LANES - 1, 1)
        m0, m1 = pltpu.roll(v0, 1, 1), pltpu.roll(v1, 1, 1)
        d0 = jnp.where(last, p1, p0) - jnp.where(first, left, m0)
        d1 = jnp.where(last, right, p1) - jnp.where(first, m0, m1)
        return d0, d1

    def edges(tile_l, tile_r, at):
        left = tile_l if at == 0 else pltpu.roll(tile_l, LANES - at, 1)
        right = pltpu.roll(tile_r, LANES - 1 - at, 1)
        return left, right

    def strength_tile(tile, zs):
        base = pl.multiple_of(tile * SUB, SUB)
        rows = pl.ds(pl.multiple_of(base + SUB, SUB), SUB)
        ahead = pl.ds(base + SUB + 1, SUB)
        behind = pl.ds(base + SUB - 1, SUB)
        tile_l, tile_r = rim_l[pl.ds(base, SUB), :], rim_r[pl.ds(base, SUB), :]
        for z in zs:
            dy_ux = along_row(
                uxy[0, z + 1, 0, rows, :], uxy[0, z + 1, 1, rows, :], *edges(tile_l, tile_r, z)
            )
            dy_uz = along_row(
                uz[z, 0, rows, :], uz[z, 1, rows, :], *edges(tile_l, tile_r, cells + z)
            )
            for h in range(2):
                dz_uy = uxy[1, z + 2, h, rows, :] - uxy[1, z, h, rows, :]
                dz_ux = uxy[0, z + 2, h, rows, :] - uxy[0, z, h, rows, :]
                dx_uz = uz[z, h, ahead, :] - uz[z, h, behind, :]
                dx_uy = uxy[1, z + 1, h, ahead, :] - uxy[1, z + 1, h, behind, :]
                cx = dy_uz[h] - dz_uy
                cy = dz_ux - dx_uz
                cz = dx_uy - dy_ux[h]
                square = cx * cx + cy * cy + cz * cz
                st[z + 1, h, rows, :] = square * (0.5 * lax.rsqrt(jnp.maximum(square, TINY)))

    def inner(tile, carry):
        strength_tile(tile, range(1, cells - 1))
        return carry

    def outer(tile, carry):
        strength_tile(tile, (0, cells - 1))
        rows = pl.ds(pl.multiple_of(tile * SUB + SUB, SUB), SUB)
        fields = [(st[z + 1, 0, rows, :], st[z + 1, 1, rows, :]) for z in range(cells)]
        collect(tile, fields, spack_l, spack_r)
        return carry

    for k in range(CHUNKS):
        for way, dst in ((0, rim_l), (1, rim_r)):
            @pl.when(from_img[way])
            def _(way=way, k=k):
                rim(way, k).wait_recv()

            @pl.when(jnp.logical_not(from_img[way]))
            def _(dst=dst, k=k):
                dst[pl.ds(k * per, per), :] = jnp.zeros((per, LANES), F32)

        lax.fori_loop(k * tiles, (k + 1) * tiles, inner, 0, unroll=2)
        for way, slot in ((0, 0), (1, cells + 1)):
            @pl.when(from_depth[way])
            def _(way=way, k=k):
                for h in range(2):
                    face(way, k, h).wait_recv()

            @pl.when(jnp.logical_not(from_depth[way]))
            def _(slot=slot, k=k):
                for h in range(2):
                    rows = pl.ds(SUB + k * per, per)
                    for c in range(2):
                        uxy[c, slot, h, rows, :] = jnp.zeros((per, LANES), F32)
                    st[slot, h, rows, :] = jnp.zeros((per, LANES), F32)

        lax.fori_loop(k * tiles, (k + 1) * tiles, outer, 0, unroll=2)
        for way in range(2):
            @pl.when(has_depth[way])
            def _(way=way, k=k):
                strength_face(way, k).start()

            @pl.when(has_img[way])
            def _(way=way, k=k):
                strength_rim(way, k).start()

    for table in tables:
        table.wait()
    knots = ext.shape[0]

    def hinges(read):
        steps = [read(k + 1) - read(k) for k in range(knots - 1)]
        return [read(0), steps[0]] + [steps[k] - steps[k - 1] for k in range(1, knots - 1)]

    dense = [g * (1.0 / layers) for g in hinges(lambda k: ext[k])]
    tints = [hinges(lambda k, c=c: emi[c, k]) for c in range(3)]

    def shade(tile, carry):
        base = pl.multiple_of(tile * SUB, SUB)
        here = pl.ds(base, SUB)
        rows = pl.ds(pl.multiple_of(base + SUB, SUB), SUB)
        ahead = pl.ds(base + SUB + 1, SUB)
        behind = pl.ds(base + SUB - 1, SUB)
        tile_l, tile_r = srim_l[here, :], srim_r[here, :]
        clear = [jnp.ones((SUB, LANES), F32)] * 2
        sums = [[None] * knots for _ in range(2)]
        for z in range(cells):
            mid = [st[z + 1, h, rows, :] for h in range(2)]
            dy = along_row(mid[0], mid[1], *edges(tile_l, tile_r, z))
            for h in range(2):
                dx = st[z + 1, h, ahead, :] - st[z + 1, h, behind, :]
                dz = st[z + 2, h, rows, :] - st[z, h, rows, :]
                square = dx * dx + dy[h] * dy[h] + dz * dz
                lean = jnp.abs(0.48 * dx + 0.6 * dy[h] + 0.64 * dz)
                shading = 0.3 + 0.7 * lean * lax.rsqrt(jnp.maximum(square, 4.0))
                level = jnp.minimum(mid[h], 4.0) * ((knots - 1) / 4.0)
                bends = [level] + [jnp.maximum(level - k, 0.0) for k in range(1, knots - 1)]
                optical = dense[0] + dense[1] * level
                for k in range(1, knots - 1):
                    optical = optical + dense[k + 1] * bends[k]
                loss = optical * (
                    1.0 - optical * (0.5 - optical * (1.0 / 6.0 - optical * (1.0 / 24.0)))
                )
                taken = clear[h] * loss
                clear[h] = clear[h] - taken
                lit = taken * shading
                terms = [lit] + [lit * b for b in bends]
                for n in range(knots):
                    sums[h][n] = terms[n] if z == 0 else sums[h][n] + terms[n]
        for h in range(2):
            at = (tile // tiles, lax.rem(tile, tiles) // 2, pl.ds(pl.multiple_of(lax.rem(tile, 2) * SUB, SUB), SUB), pl.ds(h * LANES, LANES))
            for c in range(3):
                colour = tints[c][0] * sums[h][0]
                for n in range(1, knots):
                    colour = colour + tints[c][n] * sums[h][n]
                part[(c, *at)] = colour
            part[(3, *at)] = clear[h]
        return carry

    def place(y):
        return (
            pl.ds(pl.multiple_of(y // 2 * SUB, SUB), SUB),
            pl.ds(pl.multiple_of(lax.rem(y, 2) * LANES, LANES), LANES),
        )

    def along_y(j):
        return lax.rem(gy + j, SIDE)

    def along_x(j):
        return lax.rem(gx + j, SIDE)

    def at_xy(x, y):
        return to_depth(x * SIDE + y)

    def row_piece(k, y, slot):
        return pltpu.make_async_remote_copy(
            src_ref=part.at[:, k, :, *place(y)],
            dst_ref=row_parts.at[k, slot],
            send_sem=row_send.at[k, y],
            recv_sem=row_recv.at[k, slot],
            device_id=at_xy(gx, y),
        )

    def col_piece(k, x, slot):
        return pltpu.make_async_remote_copy(
            src_ref=row_sum.at[k, x],
            dst_ref=col_parts.at[k, slot],
            send_sem=col_send.at[k, x],
            recv_sem=col_recv.at[k, slot],
            device_id=at_xy(x, gy),
        )

    def near(k, y, who):
        return pltpu.make_async_remote_copy(
            src_ref=done.at[k],
            dst_ref=out.at[:, k, gx, *place(who)],
            send_sem=near_send.at[k, y],
            recv_sem=near_recv.at[k, who],
            device_id=at_xy(gx, y),
        )

    def far(k, x, who):
        return pltpu.make_async_remote_copy(
            src_ref=out.at[:, k, who],
            dst_ref=out.at[:, k, who],
            send_sem=far_send.at[k, x],
            recv_sem=far_recv.at[k, who],
            device_id=at_xy(x, gy),
        )

    def own(k):
        return pltpu.make_async_copy(done.at[k], out.at[:, k, gx, *place(gy)], own_sem.at[k])

    others = range(1, SIDE)

    def begin(k):
        for j in others:
            row_piece(k, along_y(j), gy).start()
        row_parts[k, gy] = part[:, k, :, *place(gy)]

    def over(tiles_of):
        total = [tiles_of(0, c) for c in range(4)]
        for n in range(1, SIDE):
            for c in range(3):
                total[c] = total[c] + total[3] * tiles_of(n, c)
            total[3] = total[3] * tiles_of(n, 3)
        return total

    def merge_rows(k):
        for j in others:
            row_piece(k, gy, along_y(j)).wait_recv()
        for x in range(SIDE):
            total = over(lambda n, c, x=x: row_parts[k, n, c, x])
            for c in range(4):
                row_sum[k, x, c] = total[c]
        for j in others:
            col_piece(k, along_x(j), gx).start()
        col_parts[k, gx] = row_sum[k, gx]

    def merge_cols(k):
        for j in others:
            col_piece(k, gx, along_x(j)).wait_recv()
        total = over(lambda n, c: col_parts[k, n, c])
        for c in range(3):
            done[k, c] = total[c]
        done[k, 3] = 1.0 - total[3]
        for j in others:
            near(k, along_y(j), gy).start()
        own(k).start()

    def spread(k):
        own(k).wait()
        for j in others:
            near(k, gy, along_y(j)).wait_recv()
        for j in others:
            far(k, along_x(j), gx).start()

    for k in range(CHUNKS):
        for way, dst in ((0, srim_l), (1, srim_r)):
            @pl.when(from_depth[way])
            def _(way=way, k=k):
                strength_face(way, k).wait_recv()

            @pl.when(from_img[way])
            def _(way=way, k=k):
                strength_rim(way, k).wait_recv()

            @pl.when(jnp.logical_not(from_img[way]))
            def _(dst=dst, k=k):
                dst[pl.ds(k * per, per), :] = jnp.zeros((per, LANES), F32)

        lax.fori_loop(k * tiles, (k + 1) * tiles, shade, 0, unroll=2)
        begin(k)
        if k >= 1:
            merge_rows(k - 1)
        if k >= 2:
            merge_cols(k - 2)
        if k >= 3:
            spread(k - 3)

    for k in range(CHUNKS, CHUNKS + 3):
        if k - 1 < CHUNKS:
            merge_rows(k - 1)
        if k - 2 < CHUNKS:
            merge_cols(k - 2)
        spread(k - 3)

    for k in range(CHUNKS):
        for way in range(2):
            @pl.when(has_depth[way])
            def _(way=way, k=k):
                for h in range(2):
                    face(way, k, h).wait_send()
                strength_face(way, k).wait_send()

            @pl.when(has_img[way])
            def _(way=way, k=k):
                rim(way, k).wait_send()
                strength_rim(way, k).wait_send()

        for j in others:
            far(k, gx, along_x(j)).wait_recv()
            row_piece(k, along_y(j), gy).wait_send()
            col_piece(k, along_x(j), gx).wait_send()
            near(k, along_y(j), gy).wait_send()
            far(k, along_x(j), gx).wait_send()


def shards(velocity, emission, extinction):
    flow = velocity[:, :, 0]
    _, cells, cols, rows = flow.shape
    band = cols // CHUNKS // SIDE
    tall = cols + 2 * SUB
    dma = pltpu.SemaphoreType.DMA
    picture = pl.pallas_call(
        kernel,
        out_shape=jax.ShapeDtypeStruct((4, CHUNKS, SIDE, band, rows), F32),
        in_specs=[
            pl.BlockSpec(memory_space=pl.ANY),
            pl.BlockSpec(memory_space=pl.ANY),
            pl.BlockSpec(memory_space=pl.ANY),
        ],
        out_specs=pl.BlockSpec(memory_space=pl.ANY),
        scratch_shapes=[
            pltpu.VMEM((2, cells + 2, 2, tall, LANES), F32),
            pltpu.VMEM((cells, 2, tall, LANES), F32),
            pltpu.VMEM((cells + 2, 2, tall, LANES), F32),
        ]
        + [pltpu.VMEM((cols, LANES), F32) for _ in range(8)]
        + [
            pltpu.VMEM((4, CHUNKS, SIDE, band, rows), F32),
            pltpu.VMEM((CHUNKS, SIDE, 4, SIDE, SUB, LANES), F32),
            pltpu.VMEM((CHUNKS, SIDE, 4, SUB, LANES), F32),
            pltpu.VMEM((CHUNKS, SIDE, 4, SUB, LANES), F32),
            pltpu.VMEM((CHUNKS, 4, SUB, LANES), F32),
            pltpu.SMEM(emission.shape, F32),
            pltpu.SMEM(extinction.shape, F32),
            dma((2,)),
            dma((3, 2)),
            dma((2, CHUNKS, 2)),
            dma((2, CHUNKS, 2)),
        ]
        + [dma((2, CHUNKS)) for _ in range(6)]
        + [dma((CHUNKS, SIDE)) for _ in range(8)]
        + [dma((CHUNKS,))],
        compiler_params=pltpu.CompilerParams(
            collective_id=0, has_side_effects=True, vmem_limit_bytes=48 * 1024 * 1024
        ),
        cost_estimate=pl.CostEstimate(
            flops=100 * cells * cols * rows, bytes_accessed=8 * 1024 * 1024, transcendentals=0
        ),
        name="render",
    )(flow, emission, extinction)
    return picture.reshape(4, 1, cols, rows)


def solution(mesh):
    return jax.shard_map(
        shards,
        mesh=mesh,
        in_specs=(P(None, "depth", "img", None, None), P(), P()),
        out_specs=P(None, "img", None, None),
        check_vma=False,
    )
```

```python
import functools

import jax
import jax.numpy as jnp
from jax import lax
from jax.experimental import pallas as pl
from jax.experimental.pallas import tpu as pltpu
from jax.sharding import PartitionSpec as P

F32 = jnp.float32
LANES = 128
SUB = 8
CHUNKS = 4
LAST = CHUNKS - 1
EARLY = 3
HALVED = 2
SIDE = 4
TINY = 1.2e-38


def kernel(
    vel, table_hbm, out,
    uxy, uz, st, pack_l, pack_r, rim_l, rim_r, spack_l, spack_r, srim_l, srim_r,
    part, row_parts, row_sum, col_parts, done, parts, table,
    table_sem, loc_sem, face_send, face_recv, rim_send, rim_recv,
    sface_send, sface_recv, srim_send, srim_recv,
    row_send, row_recv, col_send, col_recv, near_send, near_recv, far_send, far_recv,
    piece_send, piece_recv, side_send, side_recv, cross_send, cross_recv, own_sem,
):
    depth = lax.axis_index("depth")
    img = lax.axis_index("img")
    depth_n = lax.axis_size("depth")
    img_n = lax.axis_size("img")
    cells = vel.shape[1]
    cols = vel.shape[2]
    per = cols // CHUNKS
    gx, gy = depth // SIDE, lax.rem(depth, SIDE)
    tiles = per // SUB
    layers = cells * depth_n

    def local(c, h):
        if c == 2:
            dst = uz.at[:, h, pl.ds(SUB, cols), :]
        else:
            dst = uxy.at[c, pl.ds(1, cells), h, pl.ds(SUB, cols), :]
        return pltpu.make_async_copy(
            vel.at[c, :, :, pl.ds(h * LANES, LANES)], dst, loc_sem.at[c, h]
        )

    for c in (0, 2, 1):
        for h in range(2):
            local(c, h).start()
    tables = pltpu.make_async_copy(table_hbm, table, table_sem)
    tables.start()

    barrier = pltpu.get_barrier_semaphore()

    def greet(j, carry):
        peer = lax.rem(depth + j, depth_n)
        pl.semaphore_signal(barrier, inc=1, device_id={"depth": peer, "img": img})
        return carry

    lax.fori_loop(1, depth_n, greet, 0)

    for step in (1, img_n - 1):
        beside = lax.rem(img + step, img_n)
        pl.semaphore_signal(barrier, inc=1, device_id={"depth": depth, "img": beside})

    zero_tile = jnp.zeros((SUB, LANES), F32)
    for z in range(cells):
        for h in range(2):
            for at in (0, cols + SUB):
                uxy[1, z + 1, h, pl.ds(at, SUB), :] = zero_tile
                uz[z, h, pl.ds(at, SUB), :] = zero_tile
                st[z + 1, h, pl.ds(at, SUB), :] = zero_tile

    pl.semaphore_wait(barrier, depth_n + 1)

    def to_depth(peer):
        return {"depth": peer, "img": img}

    def to_img(peer):
        return {"depth": depth, "img": peer}

    def face(way, k, h):
        layer, slot, peer = ((cells - 1, 0, depth + 1), (0, cells + 1, depth - 1))[way]
        return pltpu.make_async_remote_copy(
            src_ref=vel.at[pl.ds(0, 2), layer, pl.ds(k * per, per), pl.ds(h * LANES, LANES)],
            dst_ref=uxy.at[pl.ds(0, 2), slot, h, pl.ds(SUB + k * per, per), :],
            send_sem=face_send.at[way, k, h],
            recv_sem=face_recv.at[way, k, h],
            device_id=to_depth(peer),
        )

    def strength_face(way, k):
        layer, slot, peer = ((cells, 0, depth + 1), (1, cells + 1, depth - 1))[way]
        rows = pl.ds(SUB + k * per, per)
        return pltpu.make_async_remote_copy(
            src_ref=st.at[layer, :, rows, :],
            dst_ref=st.at[slot, :, rows, :],
            send_sem=sface_send.at[way, k],
            recv_sem=sface_recv.at[way, k],
            device_id=to_depth(peer),
        )

    def rim(way, k):
        src, dst, peer = ((pack_r, rim_l, img + 1), (pack_l, rim_r, img - 1))[way]
        rows = pl.ds(k * per, per)
        return pltpu.make_async_remote_copy(
            src_ref=src.at[rows, :], dst_ref=dst.at[rows, :],
            send_sem=rim_send.at[way, k], recv_sem=rim_recv.at[way, k],
            device_id=to_img(peer),
        )

    def strength_rim(way, k):
        src, dst, peer = ((spack_r, srim_l, img + 1), (spack_l, srim_r, img - 1))[way]
        rows = pl.ds(k * per, per)
        return pltpu.make_async_remote_copy(
            src_ref=src.at[rows, :], dst_ref=dst.at[rows, :],
            send_sem=srim_send.at[way, k], recv_sem=srim_recv.at[way, k],
            device_id=to_img(peer),
        )

    has_depth = (depth < depth_n - 1, depth > 0)
    from_depth = (depth > 0, depth < depth_n - 1)
    has_img = (img < img_n - 1, img > 0)
    from_img = (img > 0, img < img_n - 1)

    def send_face(k):
        for way in range(2):
            @pl.when(has_depth[way])
            def _(way=way):
                for h in range(2):
                    face(way, k, h).start()

    for k in range(EARLY):
        send_face(k)

    lane = lax.broadcasted_iota(jnp.int32, (SUB, LANES), 1)
    first = lane == 0
    last = lane == LANES - 1

    def collect(tile, fields, dst_l, dst_r):
        low = zero_tile
        high = zero_tile
        for at, (v0, v1) in enumerate(fields):
            low = jnp.where(lane == at, v0 if at == 0 else pltpu.roll(v0, at, 1), low)
            high = jnp.where(lane == at, pltpu.roll(v1, at + 1, 1), high)
        rows = pl.ds(pl.multiple_of(tile * SUB, SUB), SUB)
        dst_l[rows, :] = low
        dst_r[rows, :] = high

    for h in range(2):
        local(0, h).wait()
        local(2, h).wait()

    def pack_flow(tile, carry):
        rows = pl.ds(pl.multiple_of(tile * SUB + SUB, SUB), SUB)
        fields = [(uxy[0, z + 1, 0, rows, :], uxy[0, z + 1, 1, rows, :]) for z in range(cells)]
        fields += [(uz[z, 0, rows, :], uz[z, 1, rows, :]) for z in range(cells)]
        collect(tile, fields, pack_l, pack_r)
        return carry

    for k in range(CHUNKS):
        lax.fori_loop(k * tiles, (k + 1) * tiles, pack_flow, 0, unroll=4)
        for way in range(2):
            @pl.when(has_img[way])
            def _(way=way, k=k):
                rim(way, k).start()

    for h in range(2):
        local(1, h).wait()

    def along_row(v0, v1, left, right):
        p0, p1 = pltpu.roll(v0, LANES - 1, 1), pltpu.roll(v1, LANES - 1, 1)
        m0, m1 = pltpu.roll(v0, 1, 1), pltpu.roll(v1, 1, 1)
        d0 = jnp.where(last, p1, p0) - jnp.where(first, left, m0)
        d1 = jnp.where(last, right, p1) - jnp.where(first, m0, m1)
        return d0, d1

    def edges(tile_l, tile_r, at):
        left = tile_l if at == 0 else pltpu.roll(tile_l, LANES - at, 1)
        right = pltpu.roll(tile_r, LANES - 1 - at, 1)
        return left, right

    def strength_tile(tile, zs):
        base = pl.multiple_of(tile * SUB, SUB)
        rows = pl.ds(pl.multiple_of(base + SUB, SUB), SUB)
        ahead = pl.ds(base + SUB + 1, SUB)
        behind = pl.ds(base + SUB - 1, SUB)
        tile_l, tile_r = rim_l[pl.ds(base, SUB), :], rim_r[pl.ds(base, SUB), :]
        for z in zs:
            dy_ux = along_row(
                uxy[0, z + 1, 0, rows, :], uxy[0, z + 1, 1, rows, :], *edges(tile_l, tile_r, z)
            )
            dy_uz = along_row(
                uz[z, 0, rows, :], uz[z, 1, rows, :], *edges(tile_l, tile_r, cells + z)
            )
            for h in range(2):
                dz_uy = uxy[1, z + 2, h, rows, :] - uxy[1, z, h, rows, :]
                dz_ux = uxy[0, z + 2, h, rows, :] - uxy[0, z, h, rows, :]
                dx_uz = uz[z, h, ahead, :] - uz[z, h, behind, :]
                dx_uy = uxy[1, z + 1, h, ahead, :] - uxy[1, z + 1, h, behind, :]
                cx = dy_uz[h] - dz_uy
                cy = dz_ux - dx_uz
                cz = dx_uy - dy_ux[h]
                square = cx * cx + cy * cy + cz * cz
                st[z + 1, h, rows, :] = square * (0.5 * lax.rsqrt(jnp.maximum(square, TINY)))

    def inner(tile, carry):
        strength_tile(tile, range(1, cells - 1))
        return carry

    def outer(tile, carry):
        strength_tile(tile, (0, cells - 1))
        rows = pl.ds(pl.multiple_of(tile * SUB + SUB, SUB), SUB)
        fields = [(st[z + 1, 0, rows, :], st[z + 1, 1, rows, :]) for z in range(cells)]
        collect(tile, fields, spack_l, spack_r)
        return carry

    def inside(k):
        for way, dst in ((0, rim_l), (1, rim_r)):
            @pl.when(from_img[way])
            def _(way=way):
                rim(way, k).wait_recv()

            @pl.when(jnp.logical_not(from_img[way]))
            def _(dst=dst):
                dst[pl.ds(k * per, per), :] = jnp.zeros((per, LANES), F32)

        lax.fori_loop(k * tiles, (k + 1) * tiles, inner, 0, unroll=2)

    def faces(k):
        for way, slot in ((0, 0), (1, cells + 1)):
            @pl.when(from_depth[way])
            def _(way=way):
                for h in range(2):
                    face(way, k, h).wait_recv()

            @pl.when(jnp.logical_not(from_depth[way]))
            def _(slot=slot):
                for h in range(2):
                    rows = pl.ds(SUB + k * per, per)
                    for c in range(2):
                        uxy[c, slot, h, rows, :] = jnp.zeros((per, LANES), F32)
                    st[slot, h, rows, :] = jnp.zeros((per, LANES), F32)

        lax.fori_loop(k * tiles, (k + 1) * tiles, outer, 0, unroll=2)
        for way in range(2):
            @pl.when(has_depth[way])
            def _(way=way):
                strength_face(way, k).start()

            @pl.when(has_img[way])
            def _(way=way):
                strength_rim(way, k).start()

    tables.wait()
    knots = table.shape[1]

    def hinges(read):
        steps = [read(k + 1) - read(k) for k in range(knots - 1)]
        return [read(0), steps[0]] + [steps[k] - steps[k - 1] for k in range(1, knots - 1)]

    dense = [g * (1.0 / layers) for g in hinges(lambda k: table[3, k])]
    tints = [hinges(lambda k, c=c: table[c, k]) for c in range(3)]

    def shade(tile, carry):
        base = pl.multiple_of(tile * SUB, SUB)
        here = pl.ds(base, SUB)
        rows = pl.ds(pl.multiple_of(base + SUB, SUB), SUB)
        ahead = pl.ds(base + SUB + 1, SUB)
        behind = pl.ds(base + SUB - 1, SUB)
        tile_l, tile_r = srim_l[here, :], srim_r[here, :]
        clear = [jnp.ones((SUB, LANES), F32)] * 2
        sums = [[None] * knots for _ in range(2)]
        for z in range(cells):
            mid = [st[z + 1, h, rows, :] for h in range(2)]
            dy = along_row(mid[0], mid[1], *edges(tile_l, tile_r, z))
            for h in range(2):
                dx = st[z + 1, h, ahead, :] - st[z + 1, h, behind, :]
                dz = st[z + 2, h, rows, :] - st[z, h, rows, :]
                square = dx * dx + dy[h] * dy[h] + dz * dz
                lean = jnp.abs(0.48 * dx + 0.6 * dy[h] + 0.64 * dz)
                shading = 0.3 + 0.7 * lean * lax.rsqrt(jnp.maximum(square, 4.0))
                level = jnp.minimum(mid[h], 4.0) * ((knots - 1) / 4.0)
                bends = [level] + [jnp.maximum(level - k, 0.0) for k in range(1, knots - 1)]
                optical = dense[0] + dense[1] * level
                for k in range(1, knots - 1):
                    optical = optical + dense[k + 1] * bends[k]
                loss = optical * (
                    1.0 - optical * (0.5 - optical * (1.0 / 6.0 - optical * (1.0 / 24.0)))
                )
                taken = clear[h] * loss
                clear[h] = clear[h] - taken
                lit = taken * shading
                terms = [lit] + [lit * b for b in bends]
                for n in range(knots):
                    sums[h][n] = terms[n] if z == 0 else sums[h][n] + terms[n]
        for h in range(2):
            at = (tile // tiles, lax.rem(tile, tiles) // 2, pl.ds(pl.multiple_of(lax.rem(tile, 2) * SUB, SUB), SUB), pl.ds(h * LANES, LANES))
            for c in range(3):
                colour = tints[c][0] * sums[h][0]
                for n in range(1, knots):
                    colour = colour + tints[c][n] * sums[h][n]
                part[(c, *at)] = colour
            part[(3, *at)] = clear[h]
        return carry

    def place(y):
        return (
            pl.ds(pl.multiple_of(y // 2 * SUB, SUB), SUB),
            pl.ds(pl.multiple_of(lax.rem(y, 2) * LANES, LANES), LANES),
        )

    def along_y(j):
        return lax.rem(gy + j, SIDE)

    def along_x(j):
        return lax.rem(gx + j, SIDE)

    def at_xy(x, y):
        return to_depth(x * SIDE + y)

    def row_piece(k, y, slot):
        return pltpu.make_async_remote_copy(
            src_ref=part.at[:, k, :, *place(y)],
            dst_ref=row_parts.at[k, slot],
            send_sem=row_send.at[k, y],
            recv_sem=row_recv.at[k, slot],
            device_id=at_xy(gx, y),
        )

    def col_piece(k, x, slot):
        return pltpu.make_async_remote_copy(
            src_ref=row_sum.at[k, x],
            dst_ref=col_parts.at[k, slot],
            send_sem=col_send.at[k, x],
            recv_sem=col_recv.at[k, slot],
            device_id=at_xy(x, gy),
        )

    def near(k, y, who):
        some = pl.ds(0, 2 if k >= HALVED else 4)
        return pltpu.make_async_remote_copy(
            src_ref=done.at[k, some],
            dst_ref=out.at[some, k, gx, *place(who)],
            send_sem=near_send.at[k, y],
            recv_sem=near_recv.at[k, who],
            device_id=at_xy(gx, y),
        )

    def far(k, x, who):
        some = pl.ds(0, 2 if k >= HALVED else 4)
        return pltpu.make_async_remote_copy(
            src_ref=out.at[some, k, who],
            dst_ref=out.at[some, k, who],
            send_sem=far_send.at[k, x],
            recv_sem=far_recv.at[k, who],
            device_id=at_xy(x, gy),
        )

    def piece(to, slot):
        x, y = to // SIDE, lax.rem(to, SIDE)
        return pltpu.make_async_remote_copy(
            src_ref=part.at[:, LAST, x, *place(y)],
            dst_ref=parts.at[slot],
            send_sem=piece_send.at[to],
            recv_sem=piece_recv.at[slot],
            device_id=to_depth(to),
        )

    def side(k, x, who):
        return pltpu.make_async_remote_copy(
            src_ref=done.at[k, pl.ds(2, 2)],
            dst_ref=out.at[pl.ds(2, 2), k, who, *place(gy)],
            send_sem=side_send.at[k, x],
            recv_sem=side_recv.at[k, who],
            device_id=at_xy(x, gy),
        )

    def cross(k, y, who):
        return pltpu.make_async_remote_copy(
            src_ref=out.at[pl.ds(2, 2), k, :, *place(who)],
            dst_ref=out.at[pl.ds(2, 2), k, :, *place(who)],
            send_sem=cross_send.at[k, y],
            recv_sem=cross_recv.at[k, who],
            device_id=at_xy(gx, y),
        )

    def each_peer(act):
        def step(j, carry):
            act(lax.rem(depth + j, depth_n))
            return carry

        lax.fori_loop(1, depth_n, step, 0)

    def own(k):
        return pltpu.make_async_copy(done.at[k], out.at[:, k, gx, *place(gy)], own_sem.at[k])

    others = range(1, SIDE)

    def begin(k):
        for j in others:
            row_piece(k, along_y(j), gy).start()
        row_parts[k, gy] = part[:, k, :, *place(gy)]

    def over(tiles_of, count=SIDE):
        total = [tiles_of(0, c) for c in range(4)]
        for n in range(1, count):
            for c in range(3):
                total[c] = total[c] + total[3] * tiles_of(n, c)
            total[3] = total[3] * tiles_of(n, 3)
        return total

    def merge_rows(k):
        for j in others:
            row_piece(k, gy, along_y(j)).wait_recv()
        for x in range(SIDE):
            total = over(lambda n, c, x=x: row_parts[k, n, c, x])
            for c in range(4):
                row_sum[k, x, c] = total[c]
        for j in others:
            col_piece(k, along_x(j), gx).start()
        col_parts[k, gx] = row_sum[k, gx]

    def finish(k, total):
        for c in range(3):
            done[k, c] = total[c]
        done[k, 3] = 1.0 - total[3]
        for j in others:
            near(k, along_y(j), gy).start()
            if k >= HALVED:
                side(k, along_x(j), gx).start()
        own(k).start()

    def merge_cols(k):
        for j in others:
            col_piece(k, gx, along_x(j)).wait_recv()
        finish(k, over(lambda n, c: col_parts[k, n, c]))

    def begin_last():
        each_peer(lambda peer: piece(peer, depth).start())
        parts[depth] = part[:, LAST, gx, *place(gy)]

    def merge_last():
        each_peer(lambda peer: piece(depth, peer).wait_recv())
        finish(LAST, over(lambda n, c: parts[n, c], SIDE * SIDE))

    def spread(k):
        own(k).wait()
        for j in others:
            near(k, gy, along_y(j)).wait_recv()
        for j in others:
            far(k, along_x(j), gx).start()
        if k >= HALVED:
            for j in others:
                side(k, gx, along_x(j)).wait_recv()
            for j in others:
                cross(k, along_y(j), gy).start()

    def paint(k):
        for way, dst in ((0, srim_l), (1, srim_r)):
            @pl.when(from_depth[way])
            def _(way=way):
                strength_face(way, k).wait_recv()

            @pl.when(from_img[way])
            def _(way=way):
                strength_rim(way, k).wait_recv()

            @pl.when(jnp.logical_not(from_img[way]))
            def _(dst=dst):
                dst[pl.ds(k * per, per), :] = jnp.zeros((per, LANES), F32)

        lax.fori_loop(k * tiles, (k + 1) * tiles, shade, 0, unroll=2)

    inside(0)
    inside(1)
    faces(0)
    send_face(3)
    inside(2)
    faces(1)
    inside(3)
    faces(2)
    paint(0)
    begin(0)
    faces(3)
    paint(1)
    begin(1)
    paint(2)
    begin(2)
    merge_rows(0)
    paint(3)
    merge_cols(0)
    begin_last()
    merge_rows(1)
    merge_rows(2)
    merge_cols(1)
    spread(0)
    merge_cols(2)
    merge_last()
    spread(1)
    spread(2)
    spread(3)

    for k in range(CHUNKS):
        for way in range(2):
            @pl.when(has_depth[way])
            def _(way=way, k=k):
                for h in range(2):
                    face(way, k, h).wait_send()
                strength_face(way, k).wait_send()

            @pl.when(has_img[way])
            def _(way=way, k=k):
                rim(way, k).wait_send()
                strength_rim(way, k).wait_send()

        for j in others:
            far(k, gx, along_x(j)).wait_recv()
            if k < LAST:
                row_piece(k, along_y(j), gy).wait_send()
                col_piece(k, along_x(j), gx).wait_send()
            if k >= HALVED:
                cross(k, gy, along_y(j)).wait_recv()
                side(k, along_x(j), gx).wait_send()
                cross(k, along_y(j), gy).wait_send()
            near(k, along_y(j), gy).wait_send()
            far(k, along_x(j), gx).wait_send()
    each_peer(lambda peer: piece(peer, depth).wait_send())


def shards(velocity, emission, extinction):
    flow = velocity[:, :, 0]
    _, cells, cols, rows = flow.shape
    band = cols // CHUNKS // SIDE
    table = jnp.concatenate([emission, extinction[None]], axis=0)
    tall = cols + 2 * SUB
    dma = pltpu.SemaphoreType.DMA
    picture = pl.pallas_call(
        kernel,
        out_shape=jax.ShapeDtypeStruct((4, CHUNKS, SIDE, band, rows), F32),
        in_specs=[
            pl.BlockSpec(memory_space=pl.ANY),
            pl.BlockSpec(memory_space=pl.ANY),
        ],
        out_specs=pl.BlockSpec(memory_space=pl.ANY),
        scratch_shapes=[
            pltpu.VMEM((2, cells + 2, 2, tall, LANES), F32),
            pltpu.VMEM((cells, 2, tall, LANES), F32),
            pltpu.VMEM((cells + 2, 2, tall, LANES), F32),
        ]
        + [pltpu.VMEM((cols, LANES), F32) for _ in range(8)]
        + [
            pltpu.VMEM((4, CHUNKS, SIDE, band, rows), F32),
            pltpu.VMEM((CHUNKS, SIDE, 4, SIDE, SUB, LANES), F32),
            pltpu.VMEM((CHUNKS, SIDE, 4, SUB, LANES), F32),
            pltpu.VMEM((CHUNKS, SIDE, 4, SUB, LANES), F32),
            pltpu.VMEM((CHUNKS, 4, SUB, LANES), F32),
            pltpu.VMEM((SIDE * SIDE, 4, SUB, LANES), F32),
            pltpu.SMEM(table.shape, F32),
            dma,
            dma((3, 2)),
            dma((2, CHUNKS, 2)),
            dma((2, CHUNKS, 2)),
        ]
        + [dma((2, CHUNKS)) for _ in range(6)]
        + [dma((CHUNKS, SIDE)) for _ in range(8)]
        + [dma((SIDE * SIDE,)) for _ in range(2)]
        + [dma((CHUNKS, SIDE)) for _ in range(4)]
        + [dma((CHUNKS,))],
        compiler_params=pltpu.CompilerParams(
            collective_id=0, has_side_effects=True, vmem_limit_bytes=48 * 1024 * 1024
        ),
        cost_estimate=pl.CostEstimate(
            flops=100 * cells * cols * rows, bytes_accessed=8 * 1024 * 1024, transcendentals=0
        ),
        name="render",
    )(flow, table)
    return picture.reshape(4, 1, cols, rows)


def solution(mesh):
    return jax.shard_map(
        shards,
        mesh=mesh,
        in_specs=(P(None, "depth", "img", None, None), P(), P()),
        out_specs=P(None, "img", None, None),
        check_vma=False,
    )
```

```python
import functools

import jax
import jax.numpy as jnp
from jax import lax
from jax.experimental import pallas as pl
from jax.experimental.pallas import tpu as pltpu
from jax.sharding import PartitionSpec as P

F32 = jnp.float32
LANES = 128
SUB = 8
CHUNKS = 4
LAST = CHUNKS - 1
EARLY = 3
Y_FIRST = 2
SIDE = 4
TINY = 1.2e-38


def kernel(
    vel, emi_hbm, ext_hbm, out,
    uxy, uz, st, pack_l, pack_r, rim_l, rim_r, spack_l, spack_r, srim_l, srim_r,
    part, row_parts, row_sum, col_parts, done, parts, emi, ext,
    table_sem, loc_sem, face_send, face_recv, rim_send, rim_recv,
    sface_send, sface_recv, srim_send, srim_recv,
    row_send, row_recv, col_send, col_recv, near_send, near_recv, far_send, far_recv,
    piece_send, piece_recv, side_send, side_recv, cross_send, cross_recv, own_sem,
):
    depth = lax.axis_index("depth")
    img = lax.axis_index("img")
    depth_n = lax.axis_size("depth")
    img_n = lax.axis_size("img")
    cells = vel.shape[1]
    cols = vel.shape[2]
    per = cols // CHUNKS
    gx, gy = depth // SIDE, lax.rem(depth, SIDE)
    tiles = per // SUB
    layers = cells * depth_n

    def take(sem, like):
        pltpu.make_async_copy(like, like, sem).wait()

    def local(c, h):
        if c == 2:
            dst = uz.at[:, h, pl.ds(SUB, cols), :]
        else:
            dst = uxy.at[c, pl.ds(1, cells), h, pl.ds(SUB, cols), :]
        return pltpu.make_async_copy(
            vel.at[c, :, :, pl.ds(h * LANES, LANES)], dst, loc_sem.at[c % 2]
        )

    barrier = pltpu.get_barrier_semaphore()

    def greet(j, carry):
        peer = lax.rem(depth + j, depth_n)
        pl.semaphore_signal(barrier, inc=1, device_id={"depth": peer, "img": img})
        return carry

    lax.fori_loop(1, depth_n, greet, 0)

    for step in (1, img_n - 1):
        beside = lax.rem(img + step, img_n)
        pl.semaphore_signal(barrier, inc=1, device_id={"depth": depth, "img": beside})

    for c in (0, 2, 1):
        for h in range(2):
            local(c, h).start()
    tables = [
        pltpu.make_async_copy(emi_hbm, emi, table_sem.at[0]),
        pltpu.make_async_copy(ext_hbm, ext, table_sem.at[1]),
    ]
    for table in tables:
        table.start()

    zero_tile = jnp.zeros((SUB, LANES), F32)
    for z in range(cells):
        for h in range(2):
            for at in (0, cols + SUB):
                uxy[1, z + 1, h, pl.ds(at, SUB), :] = zero_tile
                uz[z, h, pl.ds(at, SUB), :] = zero_tile
                st[z + 1, h, pl.ds(at, SUB), :] = zero_tile

    pl.semaphore_wait(barrier, depth_n + 1)

    def to_depth(peer):
        return {"depth": peer, "img": img}

    def to_img(peer):
        return {"depth": depth, "img": peer}

    def face(way, k, h):
        layer, slot, peer = ((cells - 1, 0, depth + 1), (0, cells + 1, depth - 1))[way]
        return pltpu.make_async_remote_copy(
            src_ref=vel.at[pl.ds(0, 2), layer, pl.ds(k * per, per), pl.ds(h * LANES, LANES)],
            dst_ref=uxy.at[pl.ds(0, 2), slot, h, pl.ds(SUB + k * per, per), :],
            send_sem=face_send.at[way],
            recv_sem=face_recv.at[way, k],
            device_id=to_depth(peer),
        )

    def strength_face(way, k):
        layer, slot, peer = ((cells, 0, depth + 1), (1, cells + 1, depth - 1))[way]
        rows = pl.ds(SUB + k * per, per)
        return pltpu.make_async_remote_copy(
            src_ref=st.at[layer, :, rows, :],
            dst_ref=st.at[slot, :, rows, :],
            send_sem=sface_send.at[way],
            recv_sem=sface_recv.at[way, k],
            device_id=to_depth(peer),
        )

    def rim(way, k):
        src, dst, peer = ((pack_r, rim_l, img + 1), (pack_l, rim_r, img - 1))[way]
        rows = pl.ds(k * per, per)
        return pltpu.make_async_remote_copy(
            src_ref=src.at[rows, :], dst_ref=dst.at[rows, :],
            send_sem=rim_send.at[way], recv_sem=rim_recv.at[way, k],
            device_id=to_img(peer),
        )

    def strength_rim(way, k):
        src, dst, peer = ((spack_r, srim_l, img + 1), (spack_l, srim_r, img - 1))[way]
        rows = pl.ds(k * per, per)
        return pltpu.make_async_remote_copy(
            src_ref=src.at[rows, :], dst_ref=dst.at[rows, :],
            send_sem=srim_send.at[way], recv_sem=srim_recv.at[way, k],
            device_id=to_img(peer),
        )

    has_depth = (depth < depth_n - 1, depth > 0)
    from_depth = (depth > 0, depth < depth_n - 1)
    has_img = (img < img_n - 1, img > 0)
    from_img = (img > 0, img < img_n - 1)

    def send_face(k):
        for way in range(2):
            @pl.when(has_depth[way])
            def _(way=way):
                for h in range(2):
                    face(way, k, h).start()

    for k in range(EARLY):
        send_face(k)

    lane = lax.broadcasted_iota(jnp.int32, (SUB, LANES), 1)
    first = lane == 0
    last = lane == LANES - 1

    def collect(tile, fields, dst_l, dst_r):
        low = zero_tile
        high = zero_tile
        for at, (v0, v1) in enumerate(fields):
            low = jnp.where(lane == at, v0 if at == 0 else pltpu.roll(v0, at, 1), low)
            high = jnp.where(lane == at, pltpu.roll(v1, at + 1, 1), high)
        rows = pl.ds(pl.multiple_of(tile * SUB, SUB), SUB)
        dst_l[rows, :] = low
        dst_r[rows, :] = high

    inner_rows = pl.ds(SUB, cols)
    take(loc_sem.at[0], uxy.at[:, pl.ds(1, cells), :, inner_rows, :])

    def pack_flow(tile, carry):
        rows = pl.ds(pl.multiple_of(tile * SUB + SUB, SUB), SUB)
        fields = [(uxy[0, z + 1, 0, rows, :], uxy[0, z + 1, 1, rows, :]) for z in range(cells)]
        fields += [(uz[z, 0, rows, :], uz[z, 1, rows, :]) for z in range(cells)]
        collect(tile, fields, pack_l, pack_r)
        return carry

    for k in range(CHUNKS):
        lax.fori_loop(k * tiles, (k + 1) * tiles, pack_flow, 0, unroll=4)
        for way in range(2):
            @pl.when(has_img[way])
            def _(way=way, k=k):
                rim(way, k).start()

    take(loc_sem.at[1], uxy.at[1, pl.ds(1, cells), :, inner_rows, :])

    def along_row(v0, v1, left, right):
        p0, p1 = pltpu.roll(v0, LANES - 1, 1), pltpu.roll(v1, LANES - 1, 1)
        m0, m1 = pltpu.roll(v0, 1, 1), pltpu.roll(v1, 1, 1)
        d0 = jnp.where(last, p1, p0) - jnp.where(first, left, m0)
        d1 = jnp.where(last, right, p1) - jnp.where(first, m0, m1)
        return d0, d1

    def edges(tile_l, tile_r, at):
        left = tile_l if at == 0 else pltpu.roll(tile_l, LANES - at, 1)
        right = pltpu.roll(tile_r, LANES - 1 - at, 1)
        return left, right

    def strength_tile(tile, zs):
        base = pl.multiple_of(tile * SUB, SUB)
        rows = pl.ds(pl.multiple_of(base + SUB, SUB), SUB)
        ahead = pl.ds(base + SUB + 1, SUB)
        behind = pl.ds(base + SUB - 1, SUB)
        tile_l, tile_r = rim_l[pl.ds(base, SUB), :], rim_r[pl.ds(base, SUB), :]
        for z in zs:
            dy_ux = along_row(
                uxy[0, z + 1, 0, rows, :], uxy[0, z + 1, 1, rows, :], *edges(tile_l, tile_r, z)
            )
            dy_uz = along_row(
                uz[z, 0, rows, :], uz[z, 1, rows, :], *edges(tile_l, tile_r, cells + z)
            )
            for h in range(2):
                dz_uy = uxy[1, z + 2, h, rows, :] - uxy[1, z, h, rows, :]
                dz_ux = uxy[0, z + 2, h, rows, :] - uxy[0, z, h, rows, :]
                dx_uz = uz[z, h, ahead, :] - uz[z, h, behind, :]
                dx_uy = uxy[1, z + 1, h, ahead, :] - uxy[1, z + 1, h, behind, :]
                cx = dy_uz[h] - dz_uy
                cy = dz_ux - dx_uz
                cz = dx_uy - dy_ux[h]
                square = cx * cx + cy * cy + cz * cz
                st[z + 1, h, rows, :] = square * (0.5 * lax.rsqrt(jnp.maximum(square, TINY)))

    def inner(tile, carry):
        strength_tile(tile, range(1, cells - 1))
        return carry

    def outer(tile, carry):
        strength_tile(tile, (0, cells - 1))
        rows = pl.ds(pl.multiple_of(tile * SUB + SUB, SUB), SUB)
        fields = [(st[z + 1, 0, rows, :], st[z + 1, 1, rows, :]) for z in range(cells)]
        collect(tile, fields, spack_l, spack_r)
        return carry

    def inside(k):
        for way, dst in ((0, rim_l), (1, rim_r)):
            @pl.when(from_img[way])
            def _(way=way):
                rim(way, k).wait_recv()

            @pl.when(jnp.logical_not(from_img[way]))
            def _(dst=dst):
                dst[pl.ds(k * per, per), :] = jnp.zeros((per, LANES), F32)

        lax.fori_loop(k * tiles, (k + 1) * tiles, inner, 0, unroll=2)

    def faces(k):
        for way, slot in ((0, 0), (1, cells + 1)):
            @pl.when(from_depth[way])
            def _(way=way):
                slot = (0, cells + 1)[way]
                rows = pl.ds(SUB + k * per, per)
                take(face_recv.at[way, k], uxy.at[:, slot, :, rows, :])

            @pl.when(jnp.logical_not(from_depth[way]))
            def _(slot=slot):
                for h in range(2):
                    rows = pl.ds(SUB + k * per, per)
                    for c in range(2):
                        uxy[c, slot, h, rows, :] = jnp.zeros((per, LANES), F32)
                    st[slot, h, rows, :] = jnp.zeros((per, LANES), F32)

        lax.fori_loop(k * tiles, (k + 1) * tiles, outer, 0, unroll=2)
        for way in range(2):
            @pl.when(has_depth[way])
            def _(way=way):
                strength_face(way, k).start()

            @pl.when(has_img[way])
            def _(way=way):
                strength_rim(way, k).start()

    for table in tables:
        table.wait()
    knots = ext.shape[0]

    def hinges(read):
        steps = [read(k + 1) - read(k) for k in range(knots - 1)]
        return [read(0), steps[0]] + [steps[k] - steps[k - 1] for k in range(1, knots - 1)]

    dense = [g * (1.0 / layers) for g in hinges(lambda k: ext[k])]
    tints = [hinges(lambda k, c=c: emi[c, k]) for c in range(3)]

    def shade(tile, carry):
        base = pl.multiple_of(tile * SUB, SUB)
        here = pl.ds(base, SUB)
        rows = pl.ds(pl.multiple_of(base + SUB, SUB), SUB)
        ahead = pl.ds(base + SUB + 1, SUB)
        behind = pl.ds(base + SUB - 1, SUB)
        tile_l, tile_r = srim_l[here, :], srim_r[here, :]
        clear = [jnp.ones((SUB, LANES), F32)] * 2
        sums = [[None] * knots for _ in range(2)]
        for z in range(cells):
            mid = [st[z + 1, h, rows, :] for h in range(2)]
            dy = along_row(mid[0], mid[1], *edges(tile_l, tile_r, z))
            for h in range(2):
                dx = st[z + 1, h, ahead, :] - st[z + 1, h, behind, :]
                dz = st[z + 2, h, rows, :] - st[z, h, rows, :]
                square = dx * dx + dy[h] * dy[h] + dz * dz
                lean = jnp.abs(0.48 * dx + 0.6 * dy[h] + 0.64 * dz)
                shading = 0.3 + 0.7 * lean * lax.rsqrt(jnp.maximum(square, 4.0))
                level = jnp.minimum(mid[h], 4.0) * ((knots - 1) / 4.0)
                bends = [level] + [jnp.maximum(level - k, 0.0) for k in range(1, knots - 1)]
                optical = dense[0] + dense[1] * level
                for k in range(1, knots - 1):
                    optical = optical + dense[k + 1] * bends[k]
                loss = optical * (
                    1.0 - optical * (0.5 - optical * (1.0 / 6.0 - optical * (1.0 / 24.0)))
                )
                taken = clear[h] * loss
                clear[h] = clear[h] - taken
                lit = taken * shading
                terms = [lit] + [lit * b for b in bends]
                for n in range(knots):
                    sums[h][n] = terms[n] if z == 0 else sums[h][n] + terms[n]
        for h in range(2):
            at = (tile // tiles, lax.rem(tile, tiles) // 2, pl.ds(pl.multiple_of(lax.rem(tile, 2) * SUB, SUB), SUB), pl.ds(h * LANES, LANES))
            for c in range(3):
                colour = tints[c][0] * sums[h][0]
                for n in range(1, knots):
                    colour = colour + tints[c][n] * sums[h][n]
                part[(c, *at)] = colour
            part[(3, *at)] = clear[h]
        return carry

    def place(y):
        return (
            pl.ds(pl.multiple_of(y // 2 * SUB, SUB), SUB),
            pl.ds(pl.multiple_of(lax.rem(y, 2) * LANES, LANES), LANES),
        )

    def along_y(j):
        return lax.rem(gy + j, SIDE)

    def along_x(j):
        return lax.rem(gx + j, SIDE)

    def at_xy(x, y):
        return to_depth(x * SIDE + y)

    def row_piece(k, y, slot):
        return pltpu.make_async_remote_copy(
            src_ref=part.at[:, k, :, *place(y)],
            dst_ref=row_parts.at[k, slot],
            send_sem=row_send,
            recv_sem=row_recv.at[k],
            device_id=at_xy(gx, y),
        )

    def col_piece(k, x, slot):
        return pltpu.make_async_remote_copy(
            src_ref=row_sum.at[k, x],
            dst_ref=col_parts.at[k, slot],
            send_sem=col_send,
            recv_sem=col_recv.at[k],
            device_id=at_xy(x, gy),
        )

    def near(k, y, who):
        some = pl.ds(0, Y_FIRST)
        return pltpu.make_async_remote_copy(
            src_ref=done.at[k, some],
            dst_ref=out.at[some, k, gx, *place(who)],
            send_sem=near_send,
            recv_sem=near_recv.at[k],
            device_id=at_xy(gx, y),
        )

    def far(k, x, who):
        some = pl.ds(0, Y_FIRST)
        return pltpu.make_async_remote_copy(
            src_ref=out.at[some, k, who],
            dst_ref=out.at[some, k, who],
            send_sem=far_send,
            recv_sem=far_recv.at[k],
            device_id=at_xy(x, gy),
        )

    def piece(k, to, slot):
        x, y = to // SIDE, lax.rem(to, SIDE)
        return pltpu.make_async_remote_copy(
            src_ref=part.at[:, k, x, *place(y)],
            dst_ref=parts.at[slot],
            send_sem=piece_send,
            recv_sem=piece_recv,
            device_id=to_depth(to),
        )

    def side(k, x, who):
        some = pl.ds(Y_FIRST, 4 - Y_FIRST)
        return pltpu.make_async_remote_copy(
            src_ref=done.at[k, some],
            dst_ref=out.at[some, k, who, *place(gy)],
            send_sem=side_send,
            recv_sem=side_recv.at[k],
            device_id=at_xy(x, gy),
        )

    def cross(k, y, who):
        some = pl.ds(Y_FIRST, 4 - Y_FIRST)
        return pltpu.make_async_remote_copy(
            src_ref=out.at[some, k, :, *place(who)],
            dst_ref=out.at[some, k, :, *place(who)],
            send_sem=cross_send,
            recv_sem=cross_recv.at[k],
            device_id=at_xy(gx, y),
        )

    def each_peer(act):
        def step(j, carry):
            act(lax.rem(depth + j, depth_n))
            return carry

        lax.fori_loop(1, depth_n, step, 0)

    def own(k):
        return pltpu.make_async_copy(done.at[k], out.at[:, k, gx, *place(gy)], own_sem.at[k])

    others = range(1, SIDE)
    three = pl.ds(0, SIDE - 1)
    low, high = pl.ds(0, Y_FIRST), pl.ds(Y_FIRST, 4 - Y_FIRST)

    def begin(k):
        for j in others:
            row_piece(k, along_y(j), gy).start()
        row_parts[k, gy] = part[:, k, :, *place(gy)]

    def over(tiles_of, count=SIDE):
        total = [tiles_of(0, c) for c in range(4)]
        for n in range(1, count):
            for c in range(3):
                total[c] = total[c] + total[3] * tiles_of(n, c)
            total[3] = total[3] * tiles_of(n, 3)
        return total

    def merge_rows(k):
        take(row_recv.at[k], row_parts.at[k, three])
        for x in range(SIDE):
            total = over(lambda n, c, x=x: row_parts[k, n, c, x])
            for c in range(4):
                row_sum[k, x, c] = total[c]
        for j in others:
            col_piece(k, along_x(j), gx).start()
        col_parts[k, gx] = row_sum[k, gx]

    def finish(k, total):
        for c in range(3):
            done[k, c] = total[c]
        done[k, 3] = 1.0 - total[3]
        for j in others:
            near(k, along_y(j), gy).start()
            side(k, along_x(j), gx).start()
        own(k).start()

    def merge_cols(k):
        take(col_recv.at[k], col_parts.at[k, three])
        finish(k, over(lambda n, c: col_parts[k, n, c]))

    def begin_direct(k):
        each_peer(lambda peer: piece(k, peer, depth).start())
        parts[depth] = part[:, k, gx, *place(gy)]

    def merge_direct(k):
        take(piece_recv, parts.at[pl.ds(0, depth_n - 1)])
        finish(k, over(lambda n, c: parts[n, c], SIDE * SIDE))

    def spread(k):
        own(k).wait()
        take(near_recv.at[k], col_parts.at[0, three, low])
        for j in others:
            far(k, along_x(j), gx).start()
        take(side_recv.at[k], col_parts.at[0, three, high])
        for j in others:
            cross(k, along_y(j), gy).start()

    def paint(k):
        for way, dst in ((0, srim_l), (1, srim_r)):
            @pl.when(from_depth[way])
            def _(way=way):
                strength_face(way, k).wait_recv()

            @pl.when(from_img[way])
            def _(way=way):
                strength_rim(way, k).wait_recv()

            @pl.when(jnp.logical_not(from_img[way]))
            def _(dst=dst):
                dst[pl.ds(k * per, per), :] = jnp.zeros((per, LANES), F32)

        lax.fori_loop(k * tiles, (k + 1) * tiles, shade, 0, unroll=2)

    def settle():
        for way, slot in ((0, 0), (1, cells + 1)):
            @pl.when(has_depth[way])
            def _(way=way, slot=slot):
                take(face_send.at[way], uxy.at[:, slot, :, inner_rows, :])
                take(sface_send.at[way], st.at[slot, :, inner_rows, :])

            @pl.when(has_img[way])
            def _(way=way):
                take(rim_send.at[way], pack_l)
                take(srim_send.at[way], spack_l)

        take(row_send, row_parts.at[:, three])
        take(col_send, col_parts.at[:, three])
        take(piece_send, parts.at[pl.ds(0, depth_n - 1)])

    inside(0)
    inside(1)
    faces(0)
    send_face(3)
    inside(2)
    faces(1)
    inside(3)
    faces(2)
    paint(0)
    begin(0)
    faces(3)
    paint(1)
    begin(1)
    paint(2)
    begin(2)
    merge_rows(0)
    paint(3)
    merge_rows(1)
    merge_cols(0)
    begin_direct(3)
    merge_rows(2)
    merge_cols(1)
    spread(0)
    merge_cols(2)
    merge_direct(3)
    spread(1)
    settle()
    spread(2)
    spread(3)

    take(near_send, col_parts.at[:, :, low])
    take(side_send, col_parts.at[:, :, high])
    for k in range(CHUNKS):
        take(far_recv.at[k], out.at[low, k, three])
        take(cross_recv.at[k], out.at[high, k, three])
    take(far_send, out.at[low, :, three])
    take(cross_send, out.at[high, :, three])


def shards(velocity, emission, extinction):
    flow = velocity[:, :, 0]
    _, cells, cols, rows = flow.shape
    band = cols // CHUNKS // SIDE
    tall = cols + 2 * SUB
    dma = pltpu.SemaphoreType.DMA
    picture = pl.pallas_call(
        kernel,
        out_shape=jax.ShapeDtypeStruct((4, CHUNKS, SIDE, band, rows), F32),
        in_specs=[
            pl.BlockSpec(memory_space=pl.ANY),
            pl.BlockSpec(memory_space=pl.ANY),
            pl.BlockSpec(memory_space=pl.ANY),
        ],
        out_specs=pl.BlockSpec(memory_space=pl.ANY),
        scratch_shapes=[
            pltpu.VMEM((2, cells + 2, 2, tall, LANES), F32),
            pltpu.VMEM((cells, 2, tall, LANES), F32),
            pltpu.VMEM((cells + 2, 2, tall, LANES), F32),
        ]
        + [pltpu.VMEM((cols, LANES), F32) for _ in range(8)]
        + [
            pltpu.VMEM((4, CHUNKS, SIDE, band, rows), F32),
            pltpu.VMEM((LAST, SIDE, 4, SIDE, SUB, LANES), F32),
            pltpu.VMEM((LAST, SIDE, 4, SUB, LANES), F32),
            pltpu.VMEM((LAST, SIDE, 4, SUB, LANES), F32),
            pltpu.VMEM((CHUNKS, 4, SUB, LANES), F32),
            pltpu.VMEM((SIDE * SIDE, 4, SUB, LANES), F32),
            pltpu.SMEM(emission.shape, F32),
            pltpu.SMEM(extinction.shape, F32),
            dma((2,)),
            dma((2,)),
        ]
        + [dma((2,)), dma((2, CHUNKS))] * 4
        + [dma, dma((LAST,))] * 2
        + [dma, dma((CHUNKS,))] * 2
        + [dma, dma]
        + [dma, dma((CHUNKS,))] * 2
        + [dma((CHUNKS,))],
        compiler_params=pltpu.CompilerParams(
            collective_id=0, has_side_effects=True, vmem_limit_bytes=48 * 1024 * 1024
        ),
        cost_estimate=pl.CostEstimate(
            flops=100 * cells * cols * rows, bytes_accessed=8 * 1024 * 1024, transcendentals=0
        ),
        name="render",
    )(
        flow,
        pltpu.with_memory_space_constraint(emission, pltpu.HBM),
        pltpu.with_memory_space_constraint(extinction, pltpu.HBM),
    )
    return picture.reshape(4, 1, cols, rows)


def solution(mesh):
    return jax.shard_map(
        shards,
        mesh=mesh,
        in_specs=(P(None, "depth", "img", None, None), P(), P()),
        out_specs=P(None, "img", None, None),
        check_vma=False,
    )
```

```python
import functools

import jax
import jax.numpy as jnp
from jax import lax
from jax.experimental import pallas as pl
from jax.experimental.pallas import tpu as pltpu
from jax.sharding import PartitionSpec as P

F32 = jnp.float32
LANES = 128
SUB = 8
CHUNKS = 4
LAST = CHUNKS - 1
EARLY = 3
Y_FIRST = 2
SIDE = 4
TINY = 1.2e-38


def kernel(
    vel, emi_hbm, ext_hbm, out,
    uxy, uz, st, pack_l, pack_r, rim_l, rim_r, spack_l, spack_r, srim_l, srim_r,
    part, row_parts, row_sum, col_parts, done, parts, emi, ext,
    table_sem, loc_sem, face_send, face_recv, rim_send, rim_recv,
    sface_recv, srim_recv,
    row_send, row_recv, col_send, col_recv, near_send, near_recv, far_send, far_recv,
    piece_send, piece_recv, side_recv, own_sem,
):
    depth = lax.axis_index("depth")
    img = lax.axis_index("img")
    depth_n = lax.axis_size("depth")
    img_n = lax.axis_size("img")
    cells = vel.shape[1]
    cols = vel.shape[2]
    per = cols // CHUNKS
    gx, gy = depth // SIDE, lax.rem(depth, SIDE)
    tiles = per // SUB
    layers = cells * depth_n

    def take(sem, like):
        pltpu.make_async_copy(like, like, sem).wait()

    def local(c, h):
        if c == 2:
            dst = uz.at[:, h, pl.ds(SUB, cols), :]
        else:
            dst = uxy.at[c, pl.ds(1, cells), h, pl.ds(SUB, cols), :]
        return pltpu.make_async_copy(
            vel.at[c, :, :, pl.ds(h * LANES, LANES)], dst, loc_sem.at[c % 2]
        )

    barrier = pltpu.get_barrier_semaphore()

    def greet(j, carry):
        peer = lax.rem(depth + j, depth_n)
        pl.semaphore_signal(barrier, inc=1, device_id={"depth": peer, "img": img})
        return carry

    lax.fori_loop(1, depth_n, greet, 0)

    for step in (1, img_n - 1):
        beside = lax.rem(img + step, img_n)
        pl.semaphore_signal(barrier, inc=1, device_id={"depth": depth, "img": beside})

    for c in (0, 2, 1):
        for h in range(2):
            local(c, h).start()
    tables = [
        pltpu.make_async_copy(emi_hbm, emi, table_sem.at[0]),
        pltpu.make_async_copy(ext_hbm, ext, table_sem.at[1]),
    ]
    for table in tables:
        table.start()

    zero_tile = jnp.zeros((SUB, LANES), F32)
    for z in range(cells):
        for h in range(2):
            for at in (0, cols + SUB):
                uxy[1, z + 1, h, pl.ds(at, SUB), :] = zero_tile
                uz[z, h, pl.ds(at, SUB), :] = zero_tile
                st[z + 1, h, pl.ds(at, SUB), :] = zero_tile

    pl.semaphore_wait(barrier, depth_n + 1)

    def to_depth(peer):
        return {"depth": peer, "img": img}

    def to_img(peer):
        return {"depth": depth, "img": peer}

    def face(way, k, h):
        layer, slot, peer = ((cells - 1, 0, depth + 1), (0, cells + 1, depth - 1))[way]
        return pltpu.make_async_remote_copy(
            src_ref=vel.at[pl.ds(0, 2), layer, pl.ds(k * per, per), pl.ds(h * LANES, LANES)],
            dst_ref=uxy.at[pl.ds(0, 2), slot, h, pl.ds(SUB + k * per, per), :],
            send_sem=face_send.at[way],
            recv_sem=face_recv.at[way, k],
            device_id=to_depth(peer),
        )

    def strength_face(way, k):
        layer, slot, peer = ((cells, 0, depth + 1), (1, cells + 1, depth - 1))[way]
        rows = pl.ds(SUB + k * per, per)
        return pltpu.make_async_remote_copy(
            src_ref=st.at[layer, :, rows, :],
            dst_ref=st.at[slot, :, rows, :],
            send_sem=face_send.at[way],
            recv_sem=sface_recv.at[way, k],
            device_id=to_depth(peer),
        )

    def rim(way, k):
        src, dst, peer = ((pack_r, rim_l, img + 1), (pack_l, rim_r, img - 1))[way]
        rows = pl.ds(k * per, per)
        return pltpu.make_async_remote_copy(
            src_ref=src.at[rows, :], dst_ref=dst.at[rows, :],
            send_sem=rim_send.at[way], recv_sem=rim_recv.at[way, k],
            device_id=to_img(peer),
        )

    def strength_rim(way, k):
        src, dst, peer = ((spack_r, srim_l, img + 1), (spack_l, srim_r, img - 1))[way]
        rows = pl.ds(k * per, per)
        return pltpu.make_async_remote_copy(
            src_ref=src.at[rows, :], dst_ref=dst.at[rows, :],
            send_sem=rim_send.at[way], recv_sem=srim_recv.at[way, k],
            device_id=to_img(peer),
        )

    has_depth = (depth < depth_n - 1, depth > 0)
    from_depth = (depth > 0, depth < depth_n - 1)
    has_img = (img < img_n - 1, img > 0)
    from_img = (img > 0, img < img_n - 1)

    def send_face(k):
        for way in range(2):
            @pl.when(has_depth[way])
            def _(way=way):
                for h in range(2):
                    face(way, k, h).start()

    for k in range(EARLY):
        send_face(k)

    lane = lax.broadcasted_iota(jnp.int32, (SUB, LANES), 1)
    first = lane == 0
    last = lane == LANES - 1

    def collect(tile, fields, dst_l, dst_r):
        low = zero_tile
        high = zero_tile
        for at, (v0, v1) in enumerate(fields):
            low = jnp.where(lane == at, v0 if at == 0 else pltpu.roll(v0, at, 1), low)
            high = jnp.where(lane == at, pltpu.roll(v1, at + 1, 1), high)
        rows = pl.ds(pl.multiple_of(tile * SUB, SUB), SUB)
        dst_l[rows, :] = low
        dst_r[rows, :] = high

    inner_rows = pl.ds(SUB, cols)
    take(loc_sem.at[0], uxy.at[:, pl.ds(1, cells), :, inner_rows, :])

    def pack_flow(tile, carry):
        rows = pl.ds(pl.multiple_of(tile * SUB + SUB, SUB), SUB)
        fields = [(uxy[0, z + 1, 0, rows, :], uxy[0, z + 1, 1, rows, :]) for z in range(cells)]
        fields += [(uz[z, 0, rows, :], uz[z, 1, rows, :]) for z in range(cells)]
        collect(tile, fields, pack_l, pack_r)
        return carry

    for k in range(CHUNKS):
        lax.fori_loop(k * tiles, (k + 1) * tiles, pack_flow, 0, unroll=4)
        for way in range(2):
            @pl.when(has_img[way])
            def _(way=way, k=k):
                rim(way, k).start()

    take(loc_sem.at[1], uxy.at[1, pl.ds(1, cells), :, inner_rows, :])

    def along_row(v0, v1, left, right):
        p0, p1 = pltpu.roll(v0, LANES - 1, 1), pltpu.roll(v1, LANES - 1, 1)
        m0, m1 = pltpu.roll(v0, 1, 1), pltpu.roll(v1, 1, 1)
        d0 = jnp.where(last, p1, p0) - jnp.where(first, left, m0)
        d1 = jnp.where(last, right, p1) - jnp.where(first, m0, m1)
        return d0, d1

    def edges(tile_l, tile_r, at):
        left = tile_l if at == 0 else pltpu.roll(tile_l, LANES - at, 1)
        right = pltpu.roll(tile_r, LANES - 1 - at, 1)
        return left, right

    def strength_tile(tile, zs):
        base = pl.multiple_of(tile * SUB, SUB)
        rows = pl.ds(pl.multiple_of(base + SUB, SUB), SUB)
        ahead = pl.ds(base + SUB + 1, SUB)
        behind = pl.ds(base + SUB - 1, SUB)
        tile_l, tile_r = rim_l[pl.ds(base, SUB), :], rim_r[pl.ds(base, SUB), :]
        for z in zs:
            dy_ux = along_row(
                uxy[0, z + 1, 0, rows, :], uxy[0, z + 1, 1, rows, :], *edges(tile_l, tile_r, z)
            )
            dy_uz = along_row(
                uz[z, 0, rows, :], uz[z, 1, rows, :], *edges(tile_l, tile_r, cells + z)
            )
            for h in range(2):
                dz_uy = uxy[1, z + 2, h, rows, :] - uxy[1, z, h, rows, :]
                dz_ux = uxy[0, z + 2, h, rows, :] - uxy[0, z, h, rows, :]
                dx_uz = uz[z, h, ahead, :] - uz[z, h, behind, :]
                dx_uy = uxy[1, z + 1, h, ahead, :] - uxy[1, z + 1, h, behind, :]
                cx = dy_uz[h] - dz_uy
                cy = dz_ux - dx_uz
                cz = dx_uy - dy_ux[h]
                square = cx * cx + cy * cy + cz * cz
                st[z + 1, h, rows, :] = square * (0.5 * lax.rsqrt(jnp.maximum(square, TINY)))

    def inner(tile, carry):
        strength_tile(tile, range(1, cells - 1))
        return carry

    def outer(tile, carry):
        strength_tile(tile, (0, cells - 1))
        rows = pl.ds(pl.multiple_of(tile * SUB + SUB, SUB), SUB)
        fields = [(st[z + 1, 0, rows, :], st[z + 1, 1, rows, :]) for z in range(cells)]
        collect(tile, fields, spack_l, spack_r)
        return carry

    def inside(k):
        for way, dst in ((0, rim_l), (1, rim_r)):
            @pl.when(from_img[way])
            def _(way=way):
                rim(way, k).wait_recv()

            @pl.when(jnp.logical_not(from_img[way]))
            def _(dst=dst):
                dst[pl.ds(k * per, per), :] = jnp.zeros((per, LANES), F32)

        lax.fori_loop(k * tiles, (k + 1) * tiles, inner, 0, unroll=2)

    def faces(k):
        for way, slot in ((0, 0), (1, cells + 1)):
            @pl.when(from_depth[way])
            def _(way=way):
                slot = (0, cells + 1)[way]
                rows = pl.ds(SUB + k * per, per)
                take(face_recv.at[way, k], uxy.at[:, slot, :, rows, :])

            @pl.when(jnp.logical_not(from_depth[way]))
            def _(slot=slot):
                for h in range(2):
                    rows = pl.ds(SUB + k * per, per)
                    for c in range(2):
                        uxy[c, slot, h, rows, :] = jnp.zeros((per, LANES), F32)
                    st[slot, h, rows, :] = jnp.zeros((per, LANES), F32)

        lax.fori_loop(k * tiles, (k + 1) * tiles, outer, 0, unroll=2)
        for way in range(2):
            @pl.when(has_depth[way])
            def _(way=way):
                strength_face(way, k).start()

            @pl.when(has_img[way])
            def _(way=way):
                strength_rim(way, k).start()

    for table in tables:
        table.wait()
    knots = ext.shape[0]

    def hinges(read):
        steps = [read(k + 1) - read(k) for k in range(knots - 1)]
        return [read(0), steps[0]] + [steps[k] - steps[k - 1] for k in range(1, knots - 1)]

    dense = [g * (1.0 / layers) for g in hinges(lambda k: ext[k])]
    tints = [hinges(lambda k, c=c: emi[c, k]) for c in range(3)]

    def shade(tile, carry):
        base = pl.multiple_of(tile * SUB, SUB)
        here = pl.ds(base, SUB)
        rows = pl.ds(pl.multiple_of(base + SUB, SUB), SUB)
        ahead = pl.ds(base + SUB + 1, SUB)
        behind = pl.ds(base + SUB - 1, SUB)
        tile_l, tile_r = srim_l[here, :], srim_r[here, :]
        clear = [jnp.ones((SUB, LANES), F32)] * 2
        sums = [[None] * knots for _ in range(2)]
        for z in range(cells):
            mid = [st[z + 1, h, rows, :] for h in range(2)]
            dy = along_row(mid[0], mid[1], *edges(tile_l, tile_r, z))
            for h in range(2):
                dx = st[z + 1, h, ahead, :] - st[z + 1, h, behind, :]
                dz = st[z + 2, h, rows, :] - st[z, h, rows, :]
                square = dx * dx + dy[h] * dy[h] + dz * dz
                lean = jnp.abs(0.48 * dx + 0.6 * dy[h] + 0.64 * dz)
                shading = 0.3 + 0.7 * lean * lax.rsqrt(jnp.maximum(square, 4.0))
                level = jnp.minimum(mid[h], 4.0) * ((knots - 1) / 4.0)
                bends = [level] + [jnp.maximum(level - k, 0.0) for k in range(1, knots - 1)]
                optical = dense[0] + dense[1] * level
                for k in range(1, knots - 1):
                    optical = optical + dense[k + 1] * bends[k]
                loss = optical * (
                    1.0 - optical * (0.5 - optical * (1.0 / 6.0 - optical * (1.0 / 24.0)))
                )
                taken = clear[h] * loss
                clear[h] = clear[h] - taken
                lit = taken * shading
                terms = [lit] + [lit * b for b in bends]
                for n in range(knots):
                    sums[h][n] = terms[n] if z == 0 else sums[h][n] + terms[n]
        for h in range(2):
            at = (tile // tiles, lax.rem(tile, tiles) // 2, pl.ds(pl.multiple_of(lax.rem(tile, 2) * SUB, SUB), SUB), pl.ds(h * LANES, LANES))
            for c in range(3):
                colour = tints[c][0] * sums[h][0]
                for n in range(1, knots):
                    colour = colour + tints[c][n] * sums[h][n]
                part[(c, *at)] = colour
            part[(3, *at)] = clear[h]
        return carry

    def place(y):
        return (
            pl.ds(pl.multiple_of(y // 2 * SUB, SUB), SUB),
            pl.ds(pl.multiple_of(lax.rem(y, 2) * LANES, LANES), LANES),
        )

    def along_y(j):
        return lax.rem(gy + j, SIDE)

    def along_x(j):
        return lax.rem(gx + j, SIDE)

    def at_xy(x, y):
        return to_depth(x * SIDE + y)

    def row_piece(k, y, slot):
        return pltpu.make_async_remote_copy(
            src_ref=part.at[:, k, :, *place(y)],
            dst_ref=row_parts.at[k, slot],
            send_sem=row_send,
            recv_sem=row_recv.at[k],
            device_id=at_xy(gx, y),
        )

    def col_piece(k, x, slot):
        return pltpu.make_async_remote_copy(
            src_ref=row_sum.at[k, x],
            dst_ref=col_parts.at[k, slot],
            send_sem=col_send,
            recv_sem=col_recv.at[k],
            device_id=at_xy(x, gy),
        )

    def near(k, y, who):
        some = pl.ds(0, Y_FIRST)
        return pltpu.make_async_remote_copy(
            src_ref=done.at[k, some],
            dst_ref=out.at[some, k, gx, *place(who)],
            send_sem=near_send,
            recv_sem=near_recv.at[k],
            device_id=at_xy(gx, y),
        )

    def far(k, x, who):
        some = pl.ds(0, Y_FIRST)
        return pltpu.make_async_remote_copy(
            src_ref=out.at[some, k, who],
            dst_ref=out.at[some, k, who],
            send_sem=far_send,
            recv_sem=far_recv,
            device_id=at_xy(x, gy),
        )

    def piece(k, to, slot):
        x, y = to // SIDE, lax.rem(to, SIDE)
        return pltpu.make_async_remote_copy(
            src_ref=part.at[:, k, x, *place(y)],
            dst_ref=parts.at[slot],
            send_sem=piece_send,
            recv_sem=piece_recv,
            device_id=to_depth(to),
        )

    def side(k, x, who):
        some = pl.ds(Y_FIRST, 4 - Y_FIRST)
        return pltpu.make_async_remote_copy(
            src_ref=done.at[k, some],
            dst_ref=out.at[some, k, who, *place(gy)],
            send_sem=near_send,
            recv_sem=side_recv.at[k],
            device_id=at_xy(x, gy),
        )

    def cross(k, y, who):
        some = pl.ds(Y_FIRST, 4 - Y_FIRST)
        return pltpu.make_async_remote_copy(
            src_ref=out.at[some, k, :, *place(who)],
            dst_ref=out.at[some, k, :, *place(who)],
            send_sem=far_send,
            recv_sem=far_recv,
            device_id=at_xy(gx, y),
        )

    def each_peer(act):
        def step(j, carry):
            act(lax.rem(depth + j, depth_n))
            return carry

        lax.fori_loop(1, depth_n, step, 0)

    def own(k):
        return pltpu.make_async_copy(done.at[k], out.at[:, k, gx, *place(gy)], own_sem.at[k])

    others = range(1, SIDE)
    three = pl.ds(0, SIDE - 1)
    low, high = pl.ds(0, Y_FIRST), pl.ds(Y_FIRST, 4 - Y_FIRST)

    def begin(k):
        for j in others:
            row_piece(k, along_y(j), gy).start()
        row_parts[k, gy] = part[:, k, :, *place(gy)]

    def over(tiles_of, count=SIDE):
        total = [tiles_of(0, c) for c in range(4)]
        for n in range(1, count):
            for c in range(3):
                total[c] = total[c] + total[3] * tiles_of(n, c)
            total[3] = total[3] * tiles_of(n, 3)
        return total

    def merge_rows(k):
        take(row_recv.at[k], row_parts.at[k, three])
        for x in range(SIDE):
            total = over(lambda n, c, x=x: row_parts[k, n, c, x])
            for c in range(4):
                row_sum[k, x, c] = total[c]
        for j in others:
            col_piece(k, along_x(j), gx).start()
        col_parts[k, gx] = row_sum[k, gx]

    def finish(k, total):
        for c in range(3):
            done[k, c] = total[c]
        done[k, 3] = 1.0 - total[3]
        for j in others:
            near(k, along_y(j), gy).start()
            side(k, along_x(j), gx).start()
        own(k).start()

    def merge_cols(k):
        take(col_recv.at[k], col_parts.at[k, three])
        finish(k, over(lambda n, c: col_parts[k, n, c]))

    def begin_direct(k):
        each_peer(lambda peer: piece(k, peer, depth).start())
        parts[depth] = part[:, k, gx, *place(gy)]

    def merge_direct(k):
        take(piece_recv, parts.at[pl.ds(0, depth_n - 1)])
        finish(k, over(lambda n, c: parts[n, c], SIDE * SIDE))

    def spread(k):
        own(k).wait()
        take(near_recv.at[k], col_parts.at[0, three, low])
        for j in others:
            far(k, along_x(j), gx).start()
        take(side_recv.at[k], col_parts.at[0, three, high])
        for j in others:
            cross(k, along_y(j), gy).start()

    def paint(k):
        for way, dst in ((0, srim_l), (1, srim_r)):
            @pl.when(from_depth[way])
            def _(way=way):
                strength_face(way, k).wait_recv()

            @pl.when(from_img[way])
            def _(way=way):
                strength_rim(way, k).wait_recv()

            @pl.when(jnp.logical_not(from_img[way]))
            def _(dst=dst):
                dst[pl.ds(k * per, per), :] = jnp.zeros((per, LANES), F32)

        lax.fori_loop(k * tiles, (k + 1) * tiles, shade, 0, unroll=2)

    def settle():
        for way, slot in ((0, 0), (1, cells + 1)):
            @pl.when(has_depth[way])
            def _(way=way, slot=slot):
                take(face_send.at[way], uxy.at[0, pl.ds(0, 3), :, inner_rows, :])

            @pl.when(has_img[way])
            def _(way=way, slot=slot):
                take(rim_send.at[way], st.at[slot, :, inner_rows, :])

        take(row_send, row_parts.at[:, three])
        take(col_send, col_parts.at[:, three])
        take(piece_send, parts.at[pl.ds(0, depth_n - 1)])

    inside(0)
    inside(1)
    faces(0)
    send_face(3)
    inside(2)
    faces(1)
    inside(3)
    faces(2)
    paint(0)
    begin(0)
    faces(3)
    paint(1)
    begin(1)
    paint(2)
    begin(2)
    merge_rows(0)
    paint(3)
    merge_rows(1)
    merge_cols(0)
    begin_direct(3)
    merge_rows(2)
    merge_cols(1)
    spread(0)
    merge_cols(2)
    merge_direct(3)
    spread(1)
    settle()
    spread(2)
    spread(3)

    take(near_send, col_parts)
    take(far_recv, out.at[:, :, three])
    take(far_send, out.at[:, :, three])


def shards(velocity, emission, extinction):
    flow = velocity[:, :, 0]
    _, cells, cols, rows = flow.shape
    band = cols // CHUNKS // SIDE
    tall = cols + 2 * SUB
    dma = pltpu.SemaphoreType.DMA
    picture = pl.pallas_call(
        kernel,
        out_shape=jax.ShapeDtypeStruct((4, CHUNKS, SIDE, band, rows), F32),
        in_specs=[
            pl.BlockSpec(memory_space=pl.ANY),
            pl.BlockSpec(memory_space=pl.ANY),
            pl.BlockSpec(memory_space=pl.ANY),
        ],
        out_specs=pl.BlockSpec(memory_space=pl.ANY),
        scratch_shapes=[
            pltpu.VMEM((2, cells + 2, 2, tall, LANES), F32),
            pltpu.VMEM((cells, 2, tall, LANES), F32),
            pltpu.VMEM((cells + 2, 2, tall, LANES), F32),
        ]
        + [pltpu.VMEM((cols, LANES), F32) for _ in range(8)]
        + [
            pltpu.VMEM((4, CHUNKS, SIDE, band, rows), F32),
            pltpu.VMEM((LAST, SIDE, 4, SIDE, SUB, LANES), F32),
            pltpu.VMEM((LAST, SIDE, 4, SUB, LANES), F32),
            pltpu.VMEM((LAST, SIDE, 4, SUB, LANES), F32),
            pltpu.VMEM((CHUNKS, 4, SUB, LANES), F32),
            pltpu.VMEM((SIDE * SIDE, 4, SUB, LANES), F32),
            pltpu.SMEM(emission.shape, F32),
            pltpu.SMEM(extinction.shape, F32),
            dma((2,)),
            dma((2,)),
        ]
        + [dma((2,)), dma((2, CHUNKS))] * 2
        + [dma((2, CHUNKS))] * 2
        + [dma, dma((LAST,))] * 2
        + [dma, dma((CHUNKS,))]
        + [dma] * 4
        + [dma((CHUNKS,))] * 2,
        compiler_params=pltpu.CompilerParams(
            collective_id=0, has_side_effects=True, vmem_limit_bytes=48 * 1024 * 1024
        ),
        cost_estimate=pl.CostEstimate(
            flops=100 * cells * cols * rows, bytes_accessed=8 * 1024 * 1024, transcendentals=0
        ),
        name="render",
    )(
        flow,
        pltpu.with_memory_space_constraint(emission, pltpu.HBM),
        pltpu.with_memory_space_constraint(extinction, pltpu.HBM),
    )
    return picture.reshape(4, 1, cols, rows)


def solution(mesh):
    return jax.shard_map(
        shards,
        mesh=mesh,
        in_specs=(P(None, "depth", "img", None, None), P(), P()),
        out_specs=P(None, "img", None, None),
        check_vma=False,
    )
```
